128 devices in a mesh: row: 32 (over y, x, core), col: 4 (over z).
Axes of the slice: x: 4, y: 4, z: 4, core: 2. Of those that a mesh axis runs over, the one named last changes fastest.
Arguments:
- ray_rows: bfloat16 [16384, 10, 128], P(('row', 'col')), may hold values from -6 to 6
- targets: int32 [16384, 2], P(('row', 'col')), may hold values from 0 to 127, all different within a row; in each aligned block of 128 rows (0 to 127, 128 to 255, ...) at most 3 rows name the same one
- cell_block: int32 [16384, 2], P(('row', 'col')), may hold values from 0 to 255
- interp_weights: bfloat16 [16384, 2, 128, 128], P(('row', 'col')), may hold values from -0.5 to 0.5
- first_kernel: bfloat16 [9, 32, 10], replicated, may hold values from -0.625 to 0.625
- first_bias: float32 [32], replicated, may hold values from -3 to 3
- second_kernel: bfloat16 [9, 32, 32], replicated, may hold values from -0.375 to 0.375
- second_bias: float32 [32], replicated, may hold values from -3 to 3
Outputs:
- radar_field: bfloat16 [32, 4096, 1024], P(None, 'row', 'col')
The draws below stay inside these ranges and needn't reach their ends.
Inputs may be any that keep to these rules, and one draw needn't show every extreme that they name: The 2 targets of one piece differ. In each aligned block of 128 pieces no tile is named more than 3 times.
All inputs are finite; a program needn't handle non-finite values.
Results may differ from the reference program's by a relative error of at most 0.0054.
Values may be sent and summed in bfloat16 or wider, within the bound.
No kernel may reach another device: no remote copies, remote signals or barrier semaphores. Data moves between devices by JAX's collectives and lax.ppermute only.
A program may use at most 128 MiB of HBM per device.

```python
import math
import jax
import jax.numpy as jnp
import numpy as np
from jax import lax

F = 10
C = 32
GB = 128
CB = 128
TOP = 2
TH = 128
TW = 256
PIECE_DEV = 128
PIECES = 16384
CAP = 3
NCB = 256
N_ROW = 32
N_COL = 4
DEVICES = 128


def with_ends(values, key, smallest, top_value):
    place = [jax.random.randint(jax.random.fold_in(key, axis), (), 0, length) for axis, length in enumerate(values.shape)]
    widest = values.shape.index(max(values.shape))
    next_to = place[:widest] + [(place[widest] + 1) % values.shape[widest]] + place[widest + 1:]
    return values.at[tuple(place)].set(smallest).at[tuple(next_to)].set(top_value)


def levels(key, dims, shards, least, high):
    def one(position, parts):
        draws = jax.random.uniform(jax.random.fold_in(jax.random.fold_in(key, 6), position), (parts,), jnp.float32, least / len(shards), high / len(shards))
        return jnp.repeat(jnp.exp(draws), dims[position] // parts).reshape((-1,) + (1,) * (len(dims) - position - 1))

    factor_of = one(*shards[0])
    for cut in shards[1:]:
        factor_of = factor_of * one(*cut)
    return factor_of


def shared_out(own_key, own, number, rows, amount, top, limit, skew):
    ranking = jax.random.permutation(own_key, amount)
    crowded, usual = portions_of(amount, rows * top, limit, skew, True), portions_of(amount, rows * top, limit, skew, False)
    places = jnp.arange(amount)

    def named(lengths, offset_by):
        used = int((lengths > 0).sum())
        fixed = max(1, used // 4)
        passed = fixed + (places - fixed + offset_by * (used - fixed)) % max(1, amount - fixed)
        return jnp.zeros((amount,), jnp.int32).at[ranking[jnp.where(places < fixed, places, passed)]].set(jnp.asarray(lengths, jnp.int32))

    lengths = jnp.where(number % 4 == 0, named(crowded, number // 4), named(usual, number - number // 4 - 1))
    mixed = jax.random.permutation(jax.random.fold_in(own, 3), amount)
    giver, taker = mixed[0:amount // 2 * 2:2], mixed[1:amount // 2 * 2:2]
    slack = jnp.minimum(lengths[giver] - 1, limit - lengths[taker]) // 2
    slack = jnp.where((giver == ranking[0]) | (taker == ranking[0]) | (lengths[taker] == 0), 0, jnp.maximum(slack, 0))
    passed = jax.random.randint(jax.random.fold_in(own, 4), (amount // 2,), 0, 1 << 20) % (slack + 1)
    lengths = lengths.at[giver].add(-passed).at[taker].add(passed)
    labels = jnp.searchsorted(jnp.cumsum(lengths), jnp.arange(rows * top), side="right").astype(jnp.int32)
    grid = labels.reshape(top, rows).T
    grid = grid[jax.random.permutation(jax.random.fold_in(own, 1), rows)]
    offset_by = jax.random.randint(jax.random.fold_in(own, 2), (rows, 1), 0, top)
    return jnp.take_along_axis(grid, (jnp.arange(top)[None, :] + offset_by) % top, axis=1)


def portions_of(count, total, reach, skew, full):
    portions = [(1 << 20) // math.isqrt(grade ** skew) + 1 for grade in range(1, count + 1)]
    largest = reach if full else min(reach, max(-(-total // count), total * portions[0] // sum(portions)))
    least = 1 if total - largest >= count - 1 else 0
    holding, rest = [largest] + [least] * (count - 1), total - largest - least * (count - 1)
    while rest > 0:
        movable = [i for i in range(1, count) if holding[i] < largest] or [i for i in range(1, count) if holding[i] < reach]
        whole, remaining = sum([portions[i] for i in movable]), rest
        for i in movable:
            extra = min(reach - holding[i], max(1, remaining * portions[i] // whole), rest)
            holding[i] = holding[i] + extra
            rest = rest - extra
    return np.array(holding)


def gaussian(own_key, shape, deviation, bound, cuts=(), held_as=jnp.bfloat16):
    gain = levels(own_key, shape, cuts, -0.22, 0.18) if cuts else 1.0
    drawn = jax.random.normal(own_key, shape, jnp.float32) * deviation * gain
    return jnp.minimum(jnp.maximum(drawn, -bound), bound).astype(held_as)


def setup_inputs(seed: int = 0) -> dict:
    arg_keys = jax.random.split(jax.random.key(seed), 9)
    ray_rows = gaussian(arg_keys[0], (PIECES, F, GB), 1.0, 6.0, ((0, 128),))
    targets_keys = jax.random.split(jax.random.fold_in(arg_keys[1], 1), PIECES // PIECE_DEV)
    targets_turns = jax.random.permutation(jax.random.fold_in(arg_keys[1], 3), PIECES // PIECE_DEV)
    targets = jax.vmap(lambda own, number: shared_out(jax.random.fold_in(arg_keys[1], 2), own, number, PIECE_DEV, DEVICES, TOP, CAP, 2))(targets_keys, targets_turns).reshape((PIECES, TOP))
    cell_block = with_ends(jax.random.randint(arg_keys[2], (PIECES, TOP), 0, NCB), jax.random.fold_in(arg_keys[2], 1), 0, NCB - 1).astype(jnp.int32)
    interp_weights = gaussian(arg_keys[3], (PIECES, TOP, GB, CB), GB ** -0.5, 0.5, ((0, 128),))
    first_kernel = gaussian(arg_keys[4], (9, C, F), (9 * F) ** -0.5, 0.625)
    first_bias = gaussian(arg_keys[5], (C,), 0.5, 3.0, (), jnp.float32)
    second_kernel = gaussian(arg_keys[6], (9, C, C), (9 * C) ** -0.5, 0.375)
    second_bias = gaussian(arg_keys[7], (C,), 0.5, 3.0, (), jnp.float32)
    return dict(ray_rows=ray_rows, targets=targets, cell_block=cell_block, interp_weights=interp_weights, first_kernel=first_kernel, first_bias=first_bias, second_kernel=second_kernel, second_bias=second_bias)


def conv_taps(padded, kernel, bias, height, width):
    total = jnp.zeros((kernel.shape[1], height, width), jnp.float32)
    for tap_index in range(9):
        row_shift = tap_index // 3
        col_shift = tap_index % 3
        window = padded[:, row_shift:row_shift + height, col_shift:col_shift + width].astype(jnp.float32)
        total = total + jnp.einsum("oc,chw->ohw", kernel[tap_index].astype(jnp.float32), window)
    return jnp.maximum(total + bias[:, None, None], 0.0)


def reference(ray_rows, targets, cell_block, interp_weights, first_kernel, first_bias, second_kernel, second_bias):
    per_row = TW // CB
    grid_rows = TH * N_ROW
    grid_blocks = per_row * N_COL

    def add_group(carry, group):
        start = (group * PIECE_DEV).astype(jnp.int32)
        pieces = lax.dynamic_slice_in_dim(ray_rows, start, PIECE_DEV, 0)
        weights = lax.dynamic_slice_in_dim(interp_weights, start, PIECE_DEV, 0)
        tiles = lax.dynamic_slice_in_dim(targets, start, PIECE_DEV, 0).reshape(-1)
        blocks = lax.dynamic_slice_in_dim(cell_block, start, PIECE_DEV, 0).reshape(-1)
        values = jnp.einsum("pfg,pkgc->pkfc", pieces.astype(jnp.float32), weights.astype(jnp.float32))
        rounded = lax.optimization_barrier(values.astype(jnp.bfloat16)).astype(jnp.float32)
        grid_row = (tiles // N_COL) * TH + blocks // per_row
        grid_col = (tiles % N_COL) * per_row + blocks % per_row
        carry = carry.at[grid_row, grid_col].add(rounded.reshape(-1, F, CB))
        return carry, None

    start_grid = jnp.zeros((grid_rows, grid_blocks, F, CB), jnp.float32)
    summed, unused = lax.scan(add_group, start_grid, jnp.arange(N_ROW * N_COL, dtype=jnp.int32))
    composite = summed.transpose(2, 0, 1, 3).reshape(F, grid_rows, grid_blocks * CB).astype(jnp.bfloat16)
    grid_cols = grid_blocks * CB
    padded = jnp.pad(composite, ((0, 0), (1, 1), (1, 1)))
    hidden = conv_taps(padded, first_kernel, first_bias, grid_rows, grid_cols).astype(jnp.bfloat16)
    padded_hidden = jnp.pad(hidden, ((0, 0), (1, 1), (1, 1)))
    return conv_taps(padded_hidden, second_kernel, second_bias, grid_rows, grid_cols).astype(jnp.bfloat16)
```

```python
import jax
import jax.numpy as jnp
from jax import lax
from jax.experimental import pallas as pl
from jax.experimental.pallas import tpu as pltpu
from jax.sharding import PartitionSpec as P

F = 10
C = 32
LANES = 128
PIECES = 128
TILES = 128
TH = 128
TW = 256
CAP = 3
N_COL = 4
CHUNK = 16
FS = 16
G1 = 13
N1 = 10
G2 = 8
K1 = (G1 + 2) * 3 * FS
K2 = (G2 + 2) * 3 * C
M1 = G1 * C
M2 = G2 * C
BF = jnp.bfloat16
F32 = jnp.float32


def iota(shape, dim):
    return lax.broadcasted_iota(jnp.int32, shape, dim)


def one(mask):
    return jnp.where(mask, 1.0, 0.0).astype(BF)


def dot(a, b):
    return jnp.dot(a, b, preferred_element_type=F32)


def send_kernel(tiles_ref, blocks_ref, ray_ref, weight_ref, out_ref, vals, slab, place, pick, blockcol):
    step = pl.program_id(0)

    @pl.when(step == 0)
    def _():
        tile = jnp.concatenate([tiles_ref[0:1, :], tiles_ref[1:2, :]], axis=1)
        block = jnp.concatenate([blocks_ref[0:1, :], blocks_ref[1:2, :]], axis=1)
        pairs = 2 * PIECES
        dest = iota((TILES, pairs), 0)
        mine = dest == tile
        before = one(iota((pairs, pairs), 0) < iota((pairs, pairs), 1))
        mine_f = jnp.where(mine, 1.0, 0.0)
        slot = jnp.sum(dot(mine_f.astype(BF), before) * mine_f, axis=0, keepdims=True)
        slot = slot.astype(jnp.int32)
        right_half = block % 2 == 1
        from_left = jnp.where(right_half, tile + 1, -1)
        from_left = jnp.where(from_left % N_COL == 0, -1, from_left)
        from_right = jnp.where(right_half | (tile % N_COL == 0), -1, tile - 1)
        for s in range(CAP):
            for kind, wanted in enumerate((tile, from_left, from_right)):
                wanted = jnp.where(slot == s, wanted, -1)
                at = (kind * CAP + s) * TILES
                place[at : at + TILES, :] = one(dest == wanted)
        lane = iota((1, LANES), 1)
        within = lane % 60
        frame = (within % 20) // 2
        wanted = frame * LANES + lane % 2 + jnp.where(lane < 60, LANES - 2, 0)
        wanted = jnp.where(lane < 120, wanted, -1)
        pick[...] = one(iota((F * LANES, LANES), 0) == wanted)
        spread = jnp.where(
            iota((LANES, pairs), 0) >= 120, jnp.broadcast_to(block.astype(F32), (LANES, pairs)), 0.0
        )
        blockcol[...] = spread.T

    for i in range(CHUNK):
        both = jnp.concatenate([weight_ref[i, 0], weight_ref[i, 1]], axis=1)
        at = pl.multiple_of((step * CHUNK + i) * FS, FS)
        both = dot(ray_ref[i], both)
        for k in range(2):
            vals[k, pl.ds(at, F), :] = both[:, k * LANES : (k + 1) * LANES]

    @pl.when(step == pl.num_programs(0) - 1)
    def _():
        lane = iota((TILES, LANES), 1)
        edge = blockcol[...]
        for f2 in range(F // 2):
            columns = []
            for f in (2 * f2, 2 * f2 + 1):
                columns.append(
                    jnp.concatenate(
                        [
                            vals[k, pl.ds(f, PIECES, stride=FS), :].astype(BF)
                            for k in range(2)
                        ],
                        axis=0,
                    )
                )
            rhs = jnp.concatenate(columns, axis=1)
            edge = edge + dot(rhs, pick[2 * f2 * LANES : (2 * f2 + 2) * LANES, :])
            moved = dot(place[0 : CAP * TILES, :], rhs)
            for s in range(CAP):
                for half in range(2):
                    slab[pl.ds(s * F + 2 * f2 + half, TILES, stride=32), :] = moved[
                        s * TILES : (s + 1) * TILES, half * LANES : (half + 1) * LANES
                    ]
        moved = dot(place[...], edge.astype(BF))
        own = jnp.zeros((TILES, LANES), F32)
        beside = jnp.zeros((TILES, LANES), F32)
        for s in range(CAP):
            own = jnp.where(lane == 120 + s, moved[s * TILES : (s + 1) * TILES], own)
            left = (lane // 20 == s) | (lane == 120 + s)
            at = (CAP + s) * TILES
            beside = jnp.where(left, moved[at : at + TILES], beside)
            right = (lane // 20 == CAP + s) | (lane == 123 + s)
            at = (2 * CAP + s) * TILES
            beside = jnp.where(right, moved[at : at + TILES], beside)
        slab[pl.ds(30, TILES, stride=32), :] = own
        slab[pl.ds(31, TILES, stride=32), :] = beside
        out_ref[...] = slab[...].reshape(TILES, 32, LANES).astype(BF)


def send(tiles, blocks, ray_rows, weights):
    pairs = 2 * PIECES
    return pl.pallas_call(
        send_kernel,
        grid=(PIECES // CHUNK,),
        in_specs=[
            pl.BlockSpec((2, PIECES), lambda i: (0, 0)),
            pl.BlockSpec((2, PIECES), lambda i: (0, 0)),
            pl.BlockSpec((CHUNK, F, LANES), lambda i: (i, 0, 0)),
            pl.BlockSpec((CHUNK, 2, LANES, LANES), lambda i: (i, 0, 0, 0)),
        ],
        out_specs=pl.BlockSpec((TILES, 32, LANES), lambda i: (0, 0, 0)),
        out_shape=jax.ShapeDtypeStruct((TILES, 32, LANES), BF),
        scratch_shapes=[
            pltpu.VMEM((2, PIECES * FS, LANES), F32),
            pltpu.VMEM((TILES * 32, LANES), F32),
            pltpu.VMEM((3 * CAP * TILES, pairs), BF),
            pltpu.VMEM((F * LANES, LANES), BF),
            pltpu.VMEM((pairs, LANES), F32),
        ],
        compiler_params=pltpu.CompilerParams(vmem_limit_bytes=24 << 20),
        name="send",
    )(tiles, blocks, ray_rows, weights)


def receive_kernel(in_ref, out_ref, slab, grid_f32, halo_f32):
    slab[...] = in_ref[...].astype(F32).reshape(TILES * 32, LANES)
    own = slab[pl.ds(30, TILES, stride=32), :].T
    beside = slab[pl.ds(31, TILES, stride=32), :]
    beside_t = beside.T
    own_block = jnp.concatenate([own[120 + s : 121 + s, :] for s in range(CAP)], axis=1)
    own_block = own_block.astype(jnp.int32)
    at = (own_block % 2) * TH + own_block // 2
    spots = one(iota((2 * TH, CAP * TILES), 0) == at)
    zero = jnp.zeros((TH, LANES), F32)
    for f in range(F, FS):
        for half in range(2):
            grid_f32[half, pl.ds(f, TH, stride=FS), :] = zero
        halo_f32[pl.ds(f, TH, stride=FS), :] = zero
    lane = iota((TH, LANES), 1)
    edge_block = jnp.concatenate([beside_t[120 + s : 121 + s, :] for s in range(2 * CAP)], axis=1)
    edge_row = edge_block.astype(jnp.int32) // 2
    edge_spots = one(iota((TH, 2 * CAP * TILES), 0) == edge_row)
    edge_values = jnp.concatenate(
        [jnp.where(lane // 20 == s, beside, 0.0) for s in range(2 * CAP)], axis=0
    ).astype(BF)
    sides = dot(edge_spots, edge_values)
    left = sides + pltpu.roll(sides, LANES - 20, 1) + pltpu.roll(sides, LANES - 40, 1)
    right = pltpu.roll(left, LANES - 60, 1)
    for f2 in range(F // 2):
        rhs = jnp.concatenate(
            [
                jnp.concatenate(
                    [slab[pl.ds(s * F + f, TILES, stride=32), :].astype(BF) for s in range(CAP)],
                    axis=0,
                )
                for f in (2 * f2, 2 * f2 + 1)
            ],
            axis=1,
        )
        total = dot(spots, rhs)
        for i in range(2):
            f = 2 * f2 + i
            parts = [
                total[half * TH : (half + 1) * TH, i * LANES : (i + 1) * LANES] for half in range(2)
            ]
            for half in range(2):
                grid_f32[half, pl.ds(f, TH, stride=FS), :] = parts[half]
            l = pltpu.roll(left, (LANES - 2 * f) % LANES, 1)
            r = pltpu.roll(right, (LANES + 5 - 2 * f) % LANES, 1)
            halo = jnp.where(lane < 2, l, 0.0)
            halo = jnp.where(lane == 2, pltpu.roll(parts[0], 2, 1), halo)
            halo = jnp.where(lane == 4, pltpu.roll(parts[1], 5, 1), halo)
            halo = jnp.where((lane == 5) | (lane == 6), r, halo)
            halo_f32[pl.ds(f, TH, stride=FS), :] = halo
    for half in range(2):
        out_ref[:, :, half * LANES : (half + 1) * LANES] = (
            grid_f32[half].reshape(TH, FS, LANES).astype(BF)
        )
    out_ref[:, :, TW : TW + LANES] = halo_f32[...].reshape(TH, FS, LANES).astype(BF)


def receive(incoming):
    return pl.pallas_call(
        receive_kernel,
        out_shape=jax.ShapeDtypeStruct((TH, FS, TW + LANES), BF),
        scratch_shapes=[
            pltpu.VMEM((TILES * 32, LANES), F32),
            pltpu.VMEM((2, TH * FS, LANES), F32),
            pltpu.VMEM((TH * FS, LANES), F32),
        ],
        compiler_params=pltpu.CompilerParams(vmem_limit_bytes=24 << 20),
        name="receive",
    )(incoming)


def bands_kernel(first_ref, second_ref, one_ref, two_ref, pick_ref, rows):
    first = first_ref[...].astype(F32)
    for r in range(G1):
        moved = first if r == 0 else pltpu.roll(first, 3 * FS * r, 1)
        one_ref[r * C : (r + 1) * C, :] = moved[:, 0:K1].astype(BF)
    second = second_ref[...].astype(F32)
    for r in range(G2):
        moved = second if r == 0 else pltpu.roll(second, 3 * C * r, 1)
        for t in range(K2 // LANES + 1):
            rows[t, pl.ds(r, C, stride=G2), :] = moved[:, t * LANES : (t + 1) * LANES]
    for t in range(K2 // LANES + 1):
        width = min(LANES, K2 - t * LANES)
        two_ref[:, t * LANES : t * LANES + width] = rows[t, :, 0:width].astype(BF)
    for g in range(N1):
        lane_in = iota((LANES, LANES), 0)
        lane_out = iota((LANES, LANES), 1) - 8 * g
        for dx in range(3):
            hit = ((lane_out == 1) & (lane_in == dx)) | ((lane_out == 5) & (lane_in == 4 + dx))
            pick_ref[g * LANES : (g + 1) * LANES, dx * LANES : (dx + 1) * LANES] = one(hit)


def bands(first_kernel, second_kernel):
    first = jnp.pad(first_kernel, ((0, 0), (0, 0), (0, FS - F))).transpose(1, 0, 2)
    first = jnp.pad(first.reshape(C, 9 * FS), ((0, 0), (0, 768 - 9 * FS)))
    second = second_kernel.transpose(1, 0, 2).reshape(C, 9 * C)
    second = jnp.pad(second, ((0, 0), (0, 1024 - 9 * C)))
    return pl.pallas_call(
        bands_kernel,
        out_shape=(
            jax.ShapeDtypeStruct((M1, K1), BF),
            jax.ShapeDtypeStruct((M2, K2), BF),
            jax.ShapeDtypeStruct((N1 * LANES, 3 * LANES), BF),
        ),
        scratch_shapes=[pltpu.VMEM((8, M2, LANES), F32)],
        compiler_params=pltpu.CompilerParams(vmem_limit_bytes=24 << 20),
        cost_estimate=pl.CostEstimate(flops=0, bytes_accessed=20_000_000, transcendentals=0),
        name="bands",
    )(first, second)


def layers_kernel(
    comp_ref, above_ref, below_ref, one_ref, two_ref, pick_ref, bias1_ref, bias2_ref, out_ref, comp3, halo, hid3
):
    step = pl.program_id(0)

    @pl.when(step == 0)
    def _():
        lane = iota((FS, TW), 1)

        def shifted(rows_ref, row, to):
            x = rows_ref[row, :, 0:TW].astype(F32)
            h = rows_ref[row, :, TW : TW + LANES].astype(F32)
            h = jnp.concatenate([pltpu.roll(h, LANES - 1, 1), pltpu.roll(h, 122, 1)], axis=1)
            comp3[to, 0:FS, :] = jnp.where(lane == 0, h, pltpu.roll(x, 1, 1)).astype(BF)
            comp3[to, FS : 2 * FS, :] = rows_ref[row, :, 0:TW]
            comp3[to, 2 * FS : 3 * FS, :] = jnp.where(
                lane == TW - 1, h, pltpu.roll(x, TW - 1, 1)
            ).astype(BF)
            halo[to] = rows_ref[row, :, TW : TW + LANES]

        for i in range(2):
            shifted(above_ref, i, i)
            shifted(below_ref, i, TH + 2 + i)

        @pl.loop(0, TH, unroll=4)
        def _(row):
            shifted(comp_ref, row, row + 2)

        row_at = lax.axis_index("row")
        col_at = lax.axis_index("col")
        top = row_at == 0
        bottom = row_at == lax.axis_size("row") - 1
        first_col = col_at == 0
        last_col = col_at == lax.axis_size("col") - 1
        bias1 = jnp.broadcast_to(bias1_ref[...], (C, LANES))

        lhs = jnp.concatenate(
            [halo[g * G1 : g * G1 + G1 + 2].reshape((G1 + 2) * FS, LANES) for g in range(N1)], axis=1
        )
        packed = dot(lhs, pick_ref[...]).astype(BF)
        packed = jnp.concatenate(
            [
                packed[r * FS : (r + 1) * FS, dx * LANES : (dx + 1) * LANES]
                for r in range(G1 + 2)
                for dx in range(3)
            ],
            axis=0,
        )
        side = dot(one_ref[...], packed).reshape(G1, C, LANES) + bias1[None]
        side = jnp.maximum(side, 0.0)
        slot = iota((G1, C, LANES), 2) % 8
        side = jnp.where((slot == 1) & first_col, 0.0, side)
        side = jnp.where((slot == 5) & last_col, 0.0, side)
        side = side.reshape(M1, LANES)
        wide = iota((M1, TW), 1)
        bias1w = jnp.concatenate([bias1, bias1], axis=1)

        @pl.loop(0, N1)
        def _(g):
            window = comp3[pl.ds(g * G1, G1 + 2)].reshape(K1, TW)
            h = dot(one_ref[...], window).reshape(G1, C, TW) + bias1w[None]
            h = jnp.maximum(h, 0.0)
            h = h.reshape(M1, TW)
            e = jnp.concatenate(
                [pltpu.roll(side, 127 - 8 * g, 1), pltpu.roll(side, 122 - 8 * g, 1)], axis=1
            )
            before = jnp.where(wide == 0, e, pltpu.roll(h, 1, 1))
            after = jnp.where(wide == TW - 1, e, pltpu.roll(h, TW - 1, 1))
            for dx, x in enumerate((before, h, after)):
                hid3[pl.ds(g * G1, G1), dx * C : (dx + 1) * C, :] = x.astype(BF).reshape(G1, C, TW)

        @pl.when(top)
        def _():
            hid3[0] = jnp.zeros((3 * C, TW), BF)

        @pl.when(bottom)
        def _():
            hid3[TH + 1] = jnp.zeros((3 * C, TW), BF)

    bias2 = jnp.broadcast_to(bias2_ref[...], (M2, TW))
    halves = []
    for i in range(2):
        window = hid3[pl.ds((2 * step + i) * G2, G2 + 2)].reshape(K2, TW)
        x = dot(two_ref[...], window) + bias2
        halves.append(jnp.maximum(x, 0.0).reshape(C, G2, TW))
    out_ref[...] = jnp.concatenate(halves, axis=1).astype(BF)


def layers(comp, above, below, band1, band2, pick, bias1, bias2):
    whole = lambda a: pl.BlockSpec(a.shape, lambda i: (0,) * a.ndim)
    args = (comp, above, below, band1, band2, pick, bias1, bias2)
    return pl.pallas_call(
        layers_kernel,
        grid=(TH // (2 * G2),),
        in_specs=[whole(a) for a in args],
        out_specs=pl.BlockSpec((C, 2 * G2, TW), lambda i: (0, i, 0)),
        out_shape=jax.ShapeDtypeStruct((C, TH, TW), BF),
        scratch_shapes=[
            pltpu.VMEM((TH + 4, 3 * FS, TW), BF),
            pltpu.VMEM((TH + 4, FS, LANES), BF),
            pltpu.VMEM((TH + 2, 3 * C, TW), BF),
        ],
        compiler_params=pltpu.CompilerParams(vmem_limit_bytes=40 << 20),
        name="layers",
    )(*args)


def beside(x, axis, step):
    count = lax.axis_size(axis)
    return lax.ppermute(x, axis, [(i, i + step) for i in range(count) if 0 <= i + step < count])


def on_device(
    ray_rows,
    targets,
    cell_block,
    interp_weights,
    first_kernel,
    first_bias,
    second_kernel,
    second_bias,
):
    outgoing = send(targets.T, cell_block.T, ray_rows, interp_weights)
    incoming = lax.all_to_all(outgoing, ("row", "col"), split_axis=0, concat_axis=0, tiled=True)
    band1, band2, pick = bands(first_kernel, second_kernel)
    comp = receive(incoming)
    above = beside(comp[TH - 2 :], "row", 1)
    below = beside(comp[:2], "row", -1)
    bias1 = first_bias.reshape(C, 1)
    bias2 = jnp.broadcast_to(second_bias[:, None], (C, G2)).reshape(M2, 1)
    return layers(comp, above, below, band1, band2, pick, bias1, bias2)


def solution(mesh):
    in_specs = (
        P(("row", "col"), None, None),
        P(("row", "col"), None),
        P(("row", "col"), None),
        P(("row", "col"), None, None, None),
        P(),
        P(),
        P(),
        P(),
    )
    out_specs = P(None, "row", "col")
    return jax.shard_map(
        on_device, mesh=mesh, in_specs=in_specs, out_specs=out_specs, check_vma=False
    )
```

```python
import jax
import jax.numpy as jnp
from jax import lax
from jax.experimental import pallas as pl
from jax.experimental.pallas import tpu as pltpu
from jax.sharding import PartitionSpec as P

F = 10
C = 32
LANES = 128
PIECES = 128
TILES = 128
TH = 128
TW = 256
CAP = 3
N_COL = 4
CHUNK = 16
OUT_PARTS = 4
FS = 16
SLAB = 40
PITCH = 24
RAYS = 136
G1 = 13
N1 = 10
G2 = 8
K1 = (G1 + 2) * 3 * FS
K2 = (G2 + 2) * 3 * C
M1 = G1 * C
M2 = G2 * C
BF = jnp.bfloat16
F32 = jnp.float32


def iota(shape, dim):
    return lax.broadcasted_iota(jnp.int32, shape, dim)


def one(mask):
    return jnp.where(mask, 1.0, 0.0).astype(BF)


def dot(a, b):
    return jnp.dot(a, b, preferred_element_type=F32)


def send_kernel(
    tiles_hbm, blocks_hbm, ray_hbm, weights_ref, out_ref,
    tiles_ref, blocks_ref, ray_ref, weights, rays, vals, columns, edges, slab, place, pick, out, sems
):
    steps = PIECES // CHUNK

    def arriving(i):
        chunk = pl.ds(pl.multiple_of(i * CHUNK, CHUNK), CHUNK)
        return pltpu.make_async_copy(weights_ref.at[chunk], weights.at[chunk], sems.at[i])

    def leaving(i):
        n = TILES // OUT_PARTS
        part = pl.ds(i * n, n)
        return pltpu.make_async_copy(out.at[part], out_ref.at[part], sems.at[steps + 3 + i])

    small = [
        pltpu.make_async_copy(source, target, sems.at[steps + i])
        for i, (source, target) in enumerate(
            ((tiles_hbm, tiles_ref), (blocks_hbm, blocks_ref), (ray_hbm, ray_ref))
        )
    ]
    for copy in small:
        copy.start()
    for i in range(steps):
        arriving(i).start()

    def slots():
        tile = jnp.concatenate([tiles_ref[0:1, :], tiles_ref[1:2, :]], axis=1)
        block = jnp.concatenate([blocks_ref[0:1, :], blocks_ref[1:2, :]], axis=1)
        pairs = 2 * PIECES
        dest = iota((TILES, pairs), 0)
        mine = dest == tile
        before = one(iota((pairs, pairs), 0) < iota((pairs, pairs), 1))
        mine_f = jnp.where(mine, 1.0, 0.0)
        slot = jnp.sum(dot(mine_f.astype(BF), before) * mine_f, axis=0, keepdims=True)
        slot = slot.astype(jnp.int32)
        right_half = block % 2 == 1
        from_left = jnp.where(right_half, tile + 1, -1)
        from_left = jnp.where(from_left % N_COL == 0, -1, from_left)
        from_right = jnp.where(right_half | (tile % N_COL == 0), -1, tile - 1)
        for s in range(CAP):
            for kind, wanted in enumerate((tile, from_left, from_right)):
                wanted = jnp.where(slot == s, wanted, -1)
                at = (kind * CAP + s) * TILES
                place[at : at + TILES, :] = one(dest == wanted)
        lane = iota((1, LANES), 1)
        within = lane % 60
        frame = (within % 20) // 2
        wanted = frame * LANES + lane % 2 + jnp.where(lane < 60, LANES - 2, 0)
        wanted = jnp.where(lane < 120, wanted, -1)
        pick[...] = one(iota((F * LANES, LANES), 0) == wanted)
        spread = jnp.where(
            iota((LANES, pairs), 0) >= 120, jnp.broadcast_to(block.astype(F32), (LANES, pairs)), 0.0
        )
        edges[...] = spread.T

    small[0].wait()
    small[1].wait()
    slots()
    small[2].wait()
    for f in range(F):
        rays[f * RAYS : f * RAYS + PIECES, :] = ray_ref[f].astype(F32)

    @pl.loop(0, steps)
    def _(step):
        arriving(step).wait()
        for i in range(CHUNK):
            piece = step * CHUNK + i
            both = jnp.concatenate([weights[piece, 0], weights[piece, 1]], axis=1)
            ray = rays[pl.ds(piece, F, stride=RAYS), :].astype(BF)
            both = dot(ray, both)
            at = pl.multiple_of(piece * PITCH, 8)
            for k in range(2):
                vals[k, pl.ds(at, F), :] = both[:, k * LANES : (k + 1) * LANES]
        for k in range(2):
            to = pl.ds(pl.multiple_of(k * PIECES + step * CHUNK, CHUNK), CHUNK)
            for f in range(F):
                columns[to, f * LANES : (f + 1) * LANES] = vals[
                    k, pl.ds(step * CHUNK * PITCH + f, CHUNK, stride=PITCH), :
                ].astype(BF)

    def place_all():
        lane = iota((TILES, LANES), 1)
        for f2 in range(F // 2):
            moved = dot(place[0 : CAP * TILES, :], columns[:, 2 * f2 * LANES : (2 * f2 + 2) * LANES])
            for s in range(CAP):
                for half in range(2):
                    slab[pl.ds(s * F + 2 * f2 + half, TILES, stride=SLAB), :] = moved[
                        s * TILES : (s + 1) * TILES, half * LANES : (half + 1) * LANES
                    ]
        moved = dot(place[...], (edges[...] + dot(columns[...], pick[...])).astype(BF))
        own = jnp.zeros((TILES, LANES), F32)
        beside = jnp.zeros((TILES, LANES), F32)
        for s in range(CAP):
            own = jnp.where(lane == 120 + s, moved[s * TILES : (s + 1) * TILES], own)
            left = (lane // 20 == s) | (lane == 120 + s)
            at = (CAP + s) * TILES
            beside = jnp.where(left, moved[at : at + TILES], beside)
            right = (lane // 20 == CAP + s) | (lane == 123 + s)
            at = (2 * CAP + s) * TILES
            beside = jnp.where(right, moved[at : at + TILES], beside)
        slab[pl.ds(30, TILES, stride=SLAB), :] = own
        slab[pl.ds(31, TILES, stride=SLAB), :] = beside
        for i in range(OUT_PARTS):
            n = TILES // OUT_PARTS
            for d in range(i * n, (i + 1) * n):
                out[d] = slab[d * SLAB : d * SLAB + 32, :].astype(BF)
            leaving(i).start()
        for i in range(OUT_PARTS):
            leaving(i).wait()

    place_all()


def send(tiles, blocks, ray_rows, weights):
    pairs = 2 * PIECES
    return pl.pallas_call(
        send_kernel,
        in_specs=[pl.BlockSpec(memory_space=pl.ANY)] * 4,
        out_specs=pl.BlockSpec(memory_space=pl.ANY),
        out_shape=jax.ShapeDtypeStruct((TILES, 32, LANES), BF),
        scratch_shapes=[
            pltpu.VMEM(tiles.shape, jnp.int32),
            pltpu.VMEM(blocks.shape, jnp.int32),
            pltpu.VMEM(ray_rows.shape, BF),
            pltpu.VMEM(weights.shape, BF),
            pltpu.VMEM((F * RAYS, LANES), F32),
            pltpu.VMEM((2, PIECES * PITCH, LANES), F32),
            pltpu.VMEM((pairs, F * LANES), BF),
            pltpu.VMEM((pairs, LANES), F32),
            pltpu.VMEM((TILES * SLAB, LANES), F32),
            pltpu.VMEM((3 * CAP * TILES, pairs), BF),
            pltpu.VMEM((F * LANES, LANES), BF),
            pltpu.VMEM((TILES, 32, LANES), BF),
            pltpu.SemaphoreType.DMA((PIECES // CHUNK + 3 + OUT_PARTS,)),
        ],
        compiler_params=pltpu.CompilerParams(vmem_limit_bytes=58 << 20),
        name="send",
    )(tiles, blocks, ray_rows, weights)


def receive_kernel(in_ref, out_ref, slab, grid_f32, halo_f32):
    for d in range(TILES):
        slab[d * SLAB : d * SLAB + 32, :] = in_ref[d].astype(F32)
    own = slab[pl.ds(30, TILES, stride=SLAB), :].T
    beside = slab[pl.ds(31, TILES, stride=SLAB), :]
    beside_t = beside.T
    own_block = jnp.concatenate([own[120 + s : 121 + s, :] for s in range(CAP)], axis=1)
    own_block = own_block.astype(jnp.int32)
    at = (own_block % 2) * TH + own_block // 2
    spots = one(iota((2 * TH, CAP * TILES), 0) == at)
    zero = jnp.zeros((TH, LANES), F32)
    for f in range(F, FS):
        for half in range(2):
            grid_f32[half, pl.ds(f, TH, stride=PITCH), :] = zero
        halo_f32[pl.ds(f, TH, stride=PITCH), :] = zero
    lane = iota((TH, LANES), 1)
    edge_block = jnp.concatenate([beside_t[120 + s : 121 + s, :] for s in range(2 * CAP)], axis=1)
    edge_row = edge_block.astype(jnp.int32) // 2
    edge_spots = one(iota((TH, 2 * CAP * TILES), 0) == edge_row)
    edge_values = jnp.concatenate(
        [jnp.where(lane // 20 == s, beside, 0.0) for s in range(2 * CAP)], axis=0
    ).astype(BF)
    sides = dot(edge_spots, edge_values)
    sides = sides + pltpu.roll(sides, LANES - 20, 1) + pltpu.roll(sides, LANES - 40, 1)
    for f2 in range(F // 2):
        rhs = jnp.concatenate(
            [
                jnp.concatenate(
                    [slab[pl.ds(s * F + f, TILES, stride=SLAB), :].astype(BF) for s in range(CAP)],
                    axis=0,
                )
                for f in (2 * f2, 2 * f2 + 1)
            ],
            axis=1,
        )
        total = dot(spots, rhs)
        for i in range(2):
            f = 2 * f2 + i
            for half in range(2):
                grid_f32[half, pl.ds(f, TH, stride=PITCH), :] = total[
                    half * TH : (half + 1) * TH, i * LANES : (i + 1) * LANES
                ]
            halo = pltpu.roll(sides, LANES - 2 * f, 1) if f else sides
            halo_f32[pl.ds(f, TH, stride=PITCH), :] = halo
    for row in range(TH):
        rows = slice(row * PITCH, row * PITCH + FS)
        out_ref[row, :, 0:LANES] = grid_f32[0, rows, :].astype(BF)
        out_ref[row, :, LANES:TW] = grid_f32[1, rows, :].astype(BF)
        out_ref[row, :, TW : TW + LANES] = halo_f32[rows, :].astype(BF)


def receive(incoming):
    return pl.pallas_call(
        receive_kernel,
        out_shape=jax.ShapeDtypeStruct((TH, FS, TW + LANES), BF),
        scratch_shapes=[
            pltpu.VMEM((TILES * SLAB, LANES), F32),
            pltpu.VMEM((2, TH * PITCH, LANES), F32),
            pltpu.VMEM((TH * PITCH, LANES), F32),
        ],
        compiler_params=pltpu.CompilerParams(vmem_limit_bytes=24 << 20),
        name="receive",
    )(incoming)


def bands_kernel(first_ref, second_ref, one_ref, two_ref, rows):
    first = first_ref[...].astype(F32)
    for r in range(G1):
        moved = first if r == 0 else pltpu.roll(first, 3 * FS * r, 1)
        one_ref[r * C : (r + 1) * C, :] = moved[:, 0:K1].astype(BF)
    second = second_ref[...].astype(F32)
    for r in range(G2):
        moved = second if r == 0 else pltpu.roll(second, 3 * C * r, 1)
        for t in range(K2 // LANES + 1):
            rows[t, pl.ds(r, C, stride=G2), :] = moved[:, t * LANES : (t + 1) * LANES]
    for t in range(K2 // LANES + 1):
        width = min(LANES, K2 - t * LANES)
        two_ref[:, t * LANES : t * LANES + width] = rows[t, :, 0:width].astype(BF)


def bands(first_kernel, second_kernel):
    first = jnp.pad(first_kernel, ((0, 0), (0, 0), (0, FS - F))).transpose(1, 0, 2)
    first = jnp.pad(first.reshape(C, 9 * FS), ((0, 0), (0, 768 - 9 * FS)))
    second = second_kernel.transpose(1, 0, 2).reshape(C, 9 * C)
    second = jnp.pad(second, ((0, 0), (0, 1024 - 9 * C)))
    return pl.pallas_call(
        bands_kernel,
        out_shape=(
            jax.ShapeDtypeStruct((M1, K1), BF),
            jax.ShapeDtypeStruct((M2, K2), BF),
        ),
        scratch_shapes=[pltpu.VMEM((8, M2, LANES), F32)],
        compiler_params=pltpu.CompilerParams(vmem_limit_bytes=24 << 20),
        cost_estimate=pl.CostEstimate(flops=0, bytes_accessed=20_000_000, transcendentals=0),
        name="bands",
    )(first, second)


def layers_kernel(
    comp_ref, above_ref, below_ref, one_ref, two_ref, bias1_ref, bias2_ref, out_ref, comp3, hid3, out, sems
):
    lane = iota((FS, LANES), 1)

    def shifted(rows_ref, row, to):
        low = rows_ref[row, :, 0:LANES]
        high = rows_ref[row, :, LANES:TW]
        halo = rows_ref[row, :, TW : TW + LANES]
        low_up, high_up = pltpu.roll(low, 1, 1), pltpu.roll(high, 1, 1)
        comp3[to, 0:FS, 0:LANES] = jnp.where(lane == 0, pltpu.roll(halo, LANES - 1, 1), low_up)
        comp3[to, 0:FS, LANES:TW] = jnp.where(lane == 0, low_up, high_up)
        comp3[to, FS : 2 * FS, 0:LANES] = low
        comp3[to, FS : 2 * FS, LANES:TW] = high
        low_down, high_down = pltpu.roll(low, LANES - 1, 1), pltpu.roll(high, LANES - 1, 1)
        last = lane == LANES - 1
        comp3[to, 2 * FS : 3 * FS, 0:LANES] = jnp.where(last, high_down, low_down)
        comp3[to, 2 * FS : 3 * FS, LANES:TW] = jnp.where(
            last, pltpu.roll(halo, LANES - 1 - 60, 1), high_down
        )

    for i in range(2):
        shifted(above_ref, i, i)
        shifted(below_ref, i, TH + 2 + i)

    for row in range(TH):
        shifted(comp_ref, row, row + 2)

    row_at = lax.axis_index("row")
    col_at = lax.axis_index("col")
    top = row_at == 0
    bottom = row_at == lax.axis_size("row") - 1
    first_col = col_at == 0
    last_col = col_at == lax.axis_size("col") - 1
    bias1 = jnp.broadcast_to(bias1_ref[...], (C, LANES))

    rows = (G1 + 2) * FS
    wide = iota((rows, LANES), 1)
    halos = jnp.zeros((rows, LANES), BF)
    firsts = jnp.zeros((rows, LANES), BF)
    lasts = jnp.zeros((rows, LANES), BF)
    for g in range(N1):
        parts = []
        for row in range(g * G1, g * G1 + G1 + 2):
            ref, at = (comp_ref, row - 2)
            if row < 2:
                ref, at = above_ref, row
            if row >= TH + 2:
                ref, at = below_ref, row - TH - 2
            parts.append((ref, at))
        at = lambda lo, hi: jnp.concatenate([ref[i, :, lo:hi] for ref, i in parts], axis=0)
        halo = at(TW, TW + LANES)
        halo = pltpu.roll(halo, 2 * g, 1) if g else halo
        halos = jnp.where((wide // 2 == g) | (wide // 2 == 30 + g), halo, halos)
        low = at(0, LANES)
        low = pltpu.roll(low, 2 * g, 1) if g else low
        firsts = jnp.where(wide == 2 * g, low, firsts)
        lasts = jnp.where(wide == 60 + 2 * g, pltpu.roll(at(LANES, TW), 61 + 2 * g, 1), lasts)
    halos_down = pltpu.roll(halos, LANES - 1, 1)
    packed = (
        jnp.where(wide < 60, halos, lasts),
        jnp.where(wide < 60, halos_down, halos),
        jnp.where(wide < 60, firsts, halos_down),
    )
    packed = jnp.concatenate(
        [packed[dx][r * FS : (r + 1) * FS] for r in range(G1 + 2) for dx in range(3)], axis=0
    )
    side = dot(one_ref[...], packed).reshape(G1, C, LANES) + bias1[None]
    side = jnp.maximum(side, 0.0)
    slot = iota((G1, C, LANES), 2)
    side = jnp.where(((slot < 60) & first_col) | ((slot >= 60) & last_col), 0.0, side)
    side = side.reshape(M1, LANES).astype(BF)
    wide = iota((M1, LANES), 1)
    bias1w = jnp.concatenate([bias1, bias1], axis=1)

    for g in range(N1):
        window = comp3[pl.ds(g * G1, G1 + 2)].reshape(K1, TW)
        h = dot(one_ref[...], window).reshape(G1, C, TW) + bias1w[None]
        h = jnp.maximum(h, 0.0).reshape(M1, TW).astype(BF)
        low, high = h[:, 0:LANES], h[:, LANES:TW]
        low_up, high_up = pltpu.roll(low, 1, 1), pltpu.roll(high, 1, 1)
        low_down, high_down = pltpu.roll(low, LANES - 1, 1), pltpu.roll(high, LANES - 1, 1)
        left = pltpu.roll(side, LANES - 2 * g, 1) if g else side
        right = pltpu.roll(side, LANES - 1 - 60 - 2 * g, 1)
        first, last = wide == 0, wide == LANES - 1
        to = pl.ds(g * G1, G1)
        tiles = (
            (jnp.where(first, left, low_up), jnp.where(first, low_up, high_up)),
            (low, high),
            (jnp.where(last, high_down, low_down), jnp.where(last, right, high_down)),
        )
        for dx in range(3):
            for t in range(2):
                hid3[to, dx * C : (dx + 1) * C, t * LANES : (t + 1) * LANES] = tiles[dx][t].reshape(
                    G1, C, LANES
                )

    @pl.when(top)
    def _():
        hid3[0] = jnp.zeros((3 * C, TW), BF)

    @pl.when(bottom)
    def _():
        hid3[TH + 1] = jnp.zeros((3 * C, TW), BF)

    bias2 = jnp.broadcast_to(bias2_ref[...], (M2, TW))
    blocks = TH // (2 * G2)

    def leaving(i):
        rows = pl.ds(i * 2 * G2, 2 * G2)
        return pltpu.make_async_copy(out.at[:, rows, :], out_ref.at[:, rows, :], sems.at[i])

    for i in range(blocks):
        halves = []
        for half in range(2):
            window = hid3[pl.ds((2 * i + half) * G2, G2 + 2)].reshape(K2, TW)
            x = dot(two_ref[...], window) + bias2
            halves.append(jnp.maximum(x, 0.0).reshape(C, G2, TW))
        rows = pl.ds(i * 2 * G2, 2 * G2)
        out[:, rows, :] = jnp.concatenate(halves, axis=1).astype(BF)
        leaving(i).start()

    for i in range(blocks):
        leaving(i).wait()


def layers(comp, above, below, band1, band2, bias1, bias2):
    return pl.pallas_call(
        layers_kernel,
        out_specs=pl.BlockSpec(memory_space=pl.ANY),
        out_shape=jax.ShapeDtypeStruct((C, TH, TW), BF),
        scratch_shapes=[
            pltpu.VMEM((TH + 4, 3 * FS, TW), BF),
            pltpu.VMEM((TH + 2, 3 * C, TW), BF),
            pltpu.VMEM((C, TH, TW), BF),
            pltpu.SemaphoreType.DMA((TH // (2 * G2),)),
        ],
        compiler_params=pltpu.CompilerParams(vmem_limit_bytes=40 << 20),
        name="layers",
    )(comp, above, below, band1, band2, bias1, bias2)


def beside(x, axis, step):
    count = lax.axis_size(axis)
    return lax.ppermute(x, axis, [(i, i + step) for i in range(count) if 0 <= i + step < count])


def on_device(
    ray_rows,
    targets,
    cell_block,
    interp_weights,
    first_kernel,
    first_bias,
    second_kernel,
    second_bias,
):
    outgoing = send(targets.T, cell_block.T, ray_rows.transpose(1, 0, 2), interp_weights)
    incoming = lax.all_to_all(outgoing, ("row", "col"), split_axis=0, concat_axis=0, tiled=True)
    band1, band2 = bands(first_kernel, second_kernel)
    comp = receive(incoming)
    above = beside(comp[TH - 2 :], "row", 1)
    below = beside(comp[:2], "row", -1)
    bias1 = first_bias.reshape(C, 1)
    bias2 = jnp.broadcast_to(second_bias[:, None], (C, G2)).reshape(M2, 1)
    return layers(comp, above, below, band1, band2, bias1, bias2)


def solution(mesh):
    in_specs = (
        P(("row", "col"), None, None),
        P(("row", "col"), None),
        P(("row", "col"), None),
        P(("row", "col"), None, None, None),
        P(),
        P(),
        P(),
        P(),
    )
    out_specs = P(None, "row", "col")
    return jax.shard_map(
        on_device, mesh=mesh, in_specs=in_specs, out_specs=out_specs, check_vma=False
    )
```

```python
import jax
import jax.numpy as jnp
from jax import lax
from jax.experimental import pallas as pl
from jax.experimental.pallas import tpu as pltpu
from jax.sharding import PartitionSpec as P

F = 10
C = 32
LANES = 128
PIECES = 128
TILES = 128
TH = 128
TW = 256
CAP = 3
N_COL = 4
CHUNK = 16
OUT_PARTS = 4
FS = 16
SLAB = 40
PITCH = 24
RAYS = 136
G1 = 8
G2 = 8
EDGE = 2 * G2
RIGHT = 60
K1 = (G1 + 2) * 3 * FS
K2 = (G2 + 2) * 3 * C
M1 = G1 * C
M2 = G2 * C
BF = jnp.bfloat16
F32 = jnp.float32


def iota(shape, dim):
    return lax.broadcasted_iota(jnp.int32, shape, dim)


def one(mask):
    return jnp.where(mask, 1.0, 0.0).astype(BF)


def dot(a, b):
    return jnp.dot(a, b, preferred_element_type=F32)


def bands(first_ref, second_ref, bias_refs, one_ref, two_ref, bias_ref, taps, rows):
    taps[...] = jnp.zeros_like(taps)
    for tap in range(9):
        taps[tap * FS : tap * FS + F, 0:C] = first_ref[tap].astype(F32)
    first = taps[...].T[0:C, :]
    first = jnp.concatenate([first, jnp.zeros((C, 512 - 256), F32)], axis=1)
    for r in range(G1):
        moved = first if r == 0 else pltpu.roll(first, 3 * FS * r, 1)
        one_ref[r * C : (r + 1) * C, :] = moved[:, 0:K1].astype(BF)
    second = jnp.concatenate(
        [second_ref[tap].astype(F32) for tap in range(9)] + [jnp.zeros((C, 1024 - 9 * C), F32)], axis=1
    )
    for r in range(G2):
        moved = second if r == 0 else pltpu.roll(second, 3 * C * r, 1)
        for t in range(8):
            rows[t, pl.ds(r, C, stride=G2), :] = moved[:, t * LANES : (t + 1) * LANES]
    for t in range(8):
        width = min(LANES, K2 - t * LANES)
        two_ref[:, t * LANES : t * LANES + width] = rows[t, :, 0:width].astype(BF)
    for i, ref in enumerate(bias_refs):
        row = jnp.concatenate([ref[...], jnp.zeros((1, LANES - C), F32)], axis=1)
        bias_ref[i] = jnp.broadcast_to(row, (LANES, LANES)).T[0:C, :]


def send_kernel(
    tiles_hbm, blocks_hbm, ray_hbm, weights_ref, first_hbm, second_hbm, bias1_hbm, bias2_hbm,
    out_ref, one_hbm, two_hbm, bias_hbm,
    tiles_ref, blocks_ref, ray_ref, first_ref, second_ref, bias1_ref, bias2_ref,
    weights, rays, vals, columns, edges, slab, place, pick, out, taps, rows, one_ref, two_ref, bias_ref, sems
):
    steps = PIECES // CHUNK

    def arriving(i):
        chunk = pl.ds(pl.multiple_of(i * CHUNK, CHUNK), CHUNK)
        return pltpu.make_async_copy(weights_ref.at[chunk], weights.at[chunk], sems.at[i])

    def leaving(i):
        n = TILES // OUT_PARTS
        part = pl.ds(i * n, n)
        return pltpu.make_async_copy(out.at[part], out_ref.at[part], sems.at[steps + 10 + i])

    small = [
        pltpu.make_async_copy(source, target, sems.at[steps + i])
        for i, (source, target) in enumerate(
            (
                (tiles_hbm, tiles_ref),
                (blocks_hbm, blocks_ref),
                (ray_hbm, ray_ref),
                (first_hbm, first_ref),
                (second_hbm, second_ref),
                (bias1_hbm, bias1_ref),
                (bias2_hbm, bias2_ref),
                (one_ref, one_hbm),
                (two_ref, two_hbm),
                (bias_ref, bias_hbm),
            )
        )
    ]
    for copy in small[:7]:
        copy.start()
    for i in range(steps):
        arriving(i).start()

    def slots():
        tile = jnp.concatenate([tiles_ref[0:1, :], tiles_ref[1:2, :]], axis=1)
        block = jnp.concatenate([blocks_ref[0:1, :], blocks_ref[1:2, :]], axis=1)
        pairs = 2 * PIECES
        dest = iota((TILES, pairs), 0)
        mine = dest == tile
        before = one(iota((pairs, pairs), 0) < iota((pairs, pairs), 1))
        mine_f = jnp.where(mine, 1.0, 0.0)
        slot = jnp.sum(dot(mine_f.astype(BF), before) * mine_f, axis=0, keepdims=True)
        slot = slot.astype(jnp.int32)
        right_half = block % 2 == 1
        from_left = jnp.where(right_half, tile + 1, -1)
        from_left = jnp.where(from_left % N_COL == 0, -1, from_left)
        from_right = jnp.where(right_half | (tile % N_COL == 0), -1, tile - 1)
        for s in range(CAP):
            for kind, wanted in enumerate((tile, from_left, from_right)):
                wanted = jnp.where(slot == s, wanted, -1)
                at = (kind * CAP + s) * TILES
                place[at : at + TILES, :] = one(dest == wanted)
        lane = iota((1, LANES), 1)
        within = lane % 60
        frame = (within % 20) // 2
        wanted = frame * LANES + lane % 2 + jnp.where(lane < 60, LANES - 2, 0)
        wanted = jnp.where(lane < 120, wanted, -1)
        pick[...] = one(iota((F * LANES, LANES), 0) == wanted)
        spread = jnp.where(
            iota((LANES, pairs), 0) >= 120, jnp.broadcast_to(block.astype(F32), (LANES, pairs)), 0.0
        )
        edges[...] = spread.T

    small[0].wait()
    small[1].wait()
    slots()
    small[2].wait()
    for f in range(F):
        rays[f * RAYS : f * RAYS + PIECES, :] = ray_ref[f].astype(F32)

    for copy in small[3:7]:
        copy.wait()
    bands(first_ref, second_ref, (bias1_ref, bias2_ref), one_ref, two_ref, bias_ref, taps, rows)
    for copy in small[7:]:
        copy.start()

    @pl.loop(0, steps)
    def _(step):
        arriving(step).wait()
        for i in range(CHUNK):
            piece = step * CHUNK + i
            both = jnp.concatenate([weights[piece, 0], weights[piece, 1]], axis=1)
            ray = rays[pl.ds(piece, F, stride=RAYS), :].astype(BF)
            both = dot(ray, both)
            at = pl.multiple_of(piece * PITCH, 8)
            for k in range(2):
                vals[k, pl.ds(at, F), :] = both[:, k * LANES : (k + 1) * LANES]
        for k in range(2):
            to = pl.ds(pl.multiple_of(k * PIECES + step * CHUNK, CHUNK), CHUNK)
            for f in range(F):
                columns[to, f * LANES : (f + 1) * LANES] = vals[
                    k, pl.ds(step * CHUNK * PITCH + f, CHUNK, stride=PITCH), :
                ].astype(BF)

    def place_all():
        lane = iota((TILES, LANES), 1)
        for f2 in range(F // 2):
            moved = dot(place[0 : CAP * TILES, :], columns[:, 2 * f2 * LANES : (2 * f2 + 2) * LANES])
            for s in range(CAP):
                for half in range(2):
                    slab[pl.ds(s * F + 2 * f2 + half, TILES, stride=SLAB), :] = moved[
                        s * TILES : (s + 1) * TILES, half * LANES : (half + 1) * LANES
                    ]
        moved = dot(place[...], (edges[...] + dot(columns[...], pick[...])).astype(BF))
        own = jnp.zeros((TILES, LANES), F32)
        beside = jnp.zeros((TILES, LANES), F32)
        for s in range(CAP):
            own = jnp.where(lane == 120 + s, moved[s * TILES : (s + 1) * TILES], own)
            left = (lane // 20 == s) | (lane == 120 + s)
            at = (CAP + s) * TILES
            beside = jnp.where(left, moved[at : at + TILES], beside)
            right = (lane // 20 == CAP + s) | (lane == 123 + s)
            at = (2 * CAP + s) * TILES
            beside = jnp.where(right, moved[at : at + TILES], beside)
        slab[pl.ds(30, TILES, stride=SLAB), :] = own
        slab[pl.ds(31, TILES, stride=SLAB), :] = beside
        for i in range(OUT_PARTS):
            n = TILES // OUT_PARTS
            for d in range(i * n, (i + 1) * n):
                out[d] = slab[d * SLAB : d * SLAB + 32, :].astype(BF)
            leaving(i).start()
        for i in range(OUT_PARTS):
            leaving(i).wait()

    place_all()
    for copy in small[7:]:
        copy.wait()


def send(tiles, blocks, ray_rows, weights, first, second, bias1, bias2):
    pairs = 2 * PIECES
    return pl.pallas_call(
        send_kernel,
        in_specs=[pl.BlockSpec(memory_space=pl.ANY)] * 8,
        out_specs=[pl.BlockSpec(memory_space=pl.ANY)] * 4,
        out_shape=[
            jax.ShapeDtypeStruct((TILES, 32, LANES), BF),
            jax.ShapeDtypeStruct((M1, K1), BF),
            jax.ShapeDtypeStruct((M2, K2), BF),
            jax.ShapeDtypeStruct((2, C, LANES), F32),
        ],
        scratch_shapes=[
            pltpu.VMEM(tiles.shape, jnp.int32),
            pltpu.VMEM(blocks.shape, jnp.int32),
            pltpu.VMEM(ray_rows.shape, BF),
            pltpu.VMEM(first.shape, BF),
            pltpu.VMEM(second.shape, BF),
            pltpu.VMEM(bias1.shape, F32),
            pltpu.VMEM(bias2.shape, F32),
            pltpu.VMEM(weights.shape, BF),
            pltpu.VMEM((F * RAYS, LANES), F32),
            pltpu.VMEM((2, PIECES * PITCH, LANES), F32),
            pltpu.VMEM((pairs, F * LANES), BF),
            pltpu.VMEM((pairs, LANES), F32),
            pltpu.VMEM((TILES * SLAB, LANES), F32),
            pltpu.VMEM((3 * CAP * TILES, pairs), BF),
            pltpu.VMEM((F * LANES, LANES), BF),
            pltpu.VMEM((TILES, 32, LANES), BF),
            pltpu.VMEM((2 * LANES, LANES), F32),
            pltpu.VMEM((8, M2, LANES), F32),
            pltpu.VMEM((M1, K1), BF),
            pltpu.VMEM((M2, K2), BF),
            pltpu.VMEM((2, C, LANES), F32),
            pltpu.SemaphoreType.DMA((PIECES // CHUNK + 10 + OUT_PARTS,)),
        ],
        compiler_params=pltpu.CompilerParams(vmem_limit_bytes=58 << 20),
        name="send",
    )(tiles, blocks, ray_rows, weights, first, second, bias1, bias2)


def receive_kernel(in_ref, out_ref, near_ref, far_ref, slab, grid_f32, halo_f32):
    for d in range(TILES):
        slab[d * SLAB : d * SLAB + 32, :] = in_ref[d].astype(F32)
    own = slab[pl.ds(30, TILES, stride=SLAB), :].T
    beside = slab[pl.ds(31, TILES, stride=SLAB), :]
    beside_t = beside.T
    own_block = jnp.concatenate([own[120 + s : 121 + s, :] for s in range(CAP)], axis=1)
    own_block = own_block.astype(jnp.int32)
    at = (own_block % 2) * TH + own_block // 2
    spots = one(iota((2 * TH, CAP * TILES), 0) == at)
    zero = jnp.zeros((TH, LANES), F32)
    for f in range(F, FS):
        for half in range(2):
            grid_f32[half, pl.ds(f, TH, stride=PITCH), :] = zero
        halo_f32[pl.ds(f, TH, stride=PITCH), :] = zero
    lane = iota((TH, LANES), 1)
    edge_block = jnp.concatenate([beside_t[120 + s : 121 + s, :] for s in range(2 * CAP)], axis=1)
    edge_row = edge_block.astype(jnp.int32) // 2
    edge_spots = one(iota((TH, 2 * CAP * TILES), 0) == edge_row)
    edge_values = jnp.concatenate(
        [jnp.where(lane // 20 == s, beside, 0.0) for s in range(2 * CAP)], axis=0
    ).astype(BF)
    sides = dot(edge_spots, edge_values)
    sides = sides + pltpu.roll(sides, LANES - 20, 1) + pltpu.roll(sides, LANES - 40, 1)
    for f2 in range(F // 2):
        rhs = jnp.concatenate(
            [
                jnp.concatenate(
                    [slab[pl.ds(s * F + f, TILES, stride=SLAB), :].astype(BF) for s in range(CAP)],
                    axis=0,
                )
                for f in (2 * f2, 2 * f2 + 1)
            ],
            axis=1,
        )
        total = dot(spots, rhs)
        for i in range(2):
            f = 2 * f2 + i
            for half in range(2):
                grid_f32[half, pl.ds(f, TH, stride=PITCH), :] = total[
                    half * TH : (half + 1) * TH, i * LANES : (i + 1) * LANES
                ]
            halo = pltpu.roll(sides, LANES - 2 * f, 1) if f else sides
            halo_f32[pl.ds(f, TH, stride=PITCH), :] = halo
    for row in range(TH):
        rows = slice(row * PITCH, row * PITCH + FS)
        out_ref[row, :, 0:LANES] = grid_f32[0, rows, :].astype(BF)
        out_ref[row, :, LANES:TW] = grid_f32[1, rows, :].astype(BF)
        out_ref[row, :, TW : TW + LANES] = halo_f32[rows, :].astype(BF)

    odd = lax.axis_index("row") % 2 == 1

    @pl.when(odd)
    def _():
        near_ref[...] = out_ref[0:2]
        far_ref[...] = out_ref[TH - 2 : TH]

    @pl.when(jnp.logical_not(odd))
    def _():
        near_ref[...] = out_ref[TH - 2 : TH]
        far_ref[...] = out_ref[0:2]


def receive(incoming):
    return pl.pallas_call(
        receive_kernel,
        out_shape=[
            jax.ShapeDtypeStruct((TH, FS, TW + LANES), BF),
            jax.ShapeDtypeStruct((2, FS, TW + LANES), BF),
            jax.ShapeDtypeStruct((2, FS, TW + LANES), BF),
        ],
        scratch_shapes=[
            pltpu.VMEM((TILES * SLAB, LANES), F32),
            pltpu.VMEM((2, TH * PITCH, LANES), F32),
            pltpu.VMEM((TH * PITCH, LANES), F32),
        ],
        compiler_params=pltpu.CompilerParams(vmem_limit_bytes=24 << 20),
        name="receive",
    )(incoming)


def shifted(rows_ref, row, comp3, to):
    lane = iota((FS, LANES), 1)
    low = rows_ref[row, :, 0:LANES]
    high = rows_ref[row, :, LANES:TW]
    halo = rows_ref[row, :, TW : TW + LANES]
    low_up, high_up = pltpu.roll(low, 1, 1), pltpu.roll(high, 1, 1)
    comp3[to, 0:FS, 0:LANES] = jnp.where(lane == 0, pltpu.roll(halo, LANES - 1, 1), low_up)
    comp3[to, 0:FS, LANES:TW] = jnp.where(lane == 0, low_up, high_up)
    comp3[to, FS : 2 * FS, 0:LANES] = low
    comp3[to, FS : 2 * FS, LANES:TW] = high
    low_down, high_down = pltpu.roll(low, LANES - 1, 1), pltpu.roll(high, LANES - 1, 1)
    last = lane == LANES - 1
    comp3[to, 2 * FS : 3 * FS, 0:LANES] = jnp.where(last, high_down, low_down)
    comp3[to, 2 * FS : 3 * FS, LANES:TW] = jnp.where(
        last, pltpu.roll(halo, LANES - 1 - RIGHT, 1), high_down
    )


def first_layer_sides(groups, one_ref, bias):
    rows = (G1 + 2) * FS
    lane = iota((rows, LANES), 1)
    halos = jnp.zeros((rows, LANES), BF)
    firsts = jnp.zeros((rows, LANES), BF)
    lasts = jnp.zeros((rows, LANES), BF)
    for g, (window, _, _) in enumerate(groups):
        at = lambda lo, hi: jnp.concatenate([ref[i, :, lo:hi] for ref, i in window], axis=0)
        halo, low = at(TW, TW + LANES), at(0, LANES)
        if g:
            halo, low = pltpu.roll(halo, 2 * g, 1), pltpu.roll(low, 2 * g, 1)
        halos = jnp.where((lane // 2 == g) | (lane // 2 == RIGHT // 2 + g), halo, halos)
        firsts = jnp.where(lane == 2 * g, low, firsts)
        lasts = jnp.where(lane == RIGHT + 2 * g, pltpu.roll(at(LANES, TW), RIGHT + 1 + 2 * g, 1), lasts)
    halos_down = pltpu.roll(halos, LANES - 1, 1)
    packed = (
        jnp.where(lane < RIGHT, halos, lasts),
        jnp.where(lane < RIGHT, halos_down, halos),
        jnp.where(lane < RIGHT, firsts, halos_down),
    )
    packed = jnp.concatenate(
        [packed[dx][r * FS : (r + 1) * FS] for r in range(G1 + 2) for dx in range(3)], axis=0
    )
    side = dot(one_ref[...], packed).reshape(G1, C, LANES) + bias[None]
    side = jnp.maximum(side, 0.0)
    col_at = lax.axis_index("col")
    first_col = col_at == 0
    last_col = col_at == lax.axis_size("col") - 1
    lane = iota((G1, C, LANES), 2)
    side = jnp.where(((lane < RIGHT) & first_col) | ((lane >= RIGHT) & last_col), 0.0, side)
    return side.reshape(M1, LANES).astype(BF)


def first_layer(groups, one_ref, bias_ref, comp3, hid3):
    bias = bias_ref[0]
    wide_bias = jnp.concatenate([bias, bias], axis=1)[None]
    side = first_layer_sides(groups, one_ref, bias)
    lane = iota((M1, LANES), 1)
    first, last = lane == 0, lane == LANES - 1
    for g, (_, start, to) in enumerate(groups):
        window = comp3[start : start + G1 + 2].reshape(K1, TW)
        h = dot(one_ref[...], window).reshape(G1, C, TW) + wide_bias
        h = jnp.maximum(h, 0.0).reshape(M1, TW).astype(BF)
        low, high = h[:, 0:LANES], h[:, LANES:TW]
        low_up, high_up = pltpu.roll(low, 1, 1), pltpu.roll(high, 1, 1)
        low_down, high_down = pltpu.roll(low, LANES - 1, 1), pltpu.roll(high, LANES - 1, 1)
        left = pltpu.roll(side, LANES - 2 * g, 1) if g else side
        right = pltpu.roll(side, LANES - 1 - RIGHT - 2 * g, 1)
        tiles = (
            (jnp.where(first, left, low_up), jnp.where(first, low_up, high_up)),
            (low, high),
            (jnp.where(last, high_down, low_down), jnp.where(last, right, high_down)),
        )
        for dx in range(3):
            for t in range(2):
                hid3[to : to + G1, dx * C : (dx + 1) * C, t * LANES : (t + 1) * LANES] = tiles[dx][
                    t
                ].reshape(G1, C, LANES)


def second_layer(blocks, two_ref, bias_ref, hid3, out, out_ref, sems):
    bias = jnp.broadcast_to(bias_ref[1][:, None, :], (C, G2, LANES))
    bias = jnp.concatenate([bias, bias], axis=2)
    copies = []
    for i, (start, row) in enumerate(blocks):
        halves = []
        for half in range(2):
            at = start + half * G2
            x = dot(two_ref[...], hid3[at : at + G2 + 2].reshape(K2, TW))
            halves.append(jnp.maximum(x.reshape(C, G2, TW) + bias, 0.0))
        part = out.at[:, i * 2 * G2 : (i + 1) * 2 * G2, :]
        part[...] = jnp.concatenate(halves, axis=1).astype(BF)
        copy = pltpu.make_async_copy(part, out_ref.at[:, row : row + 2 * G2, :], sems.at[i])
        copy.start()
        copies.append(copy)
    for copy in copies:
        copy.wait()


def group_starts(count):
    return [*range(0, count - G1, G1), count - G1]


def inner_kernel(comp_ref, one_ref, two_ref, bias_ref, out_ref, comp3, hid3, out, sems):
    top, count = EDGE - 2, TH - 2 * EDGE + 4
    for i in range(count):
        shifted(comp_ref, top + i, comp3, i)
    groups = [
        ([(comp_ref, top + s + i) for i in range(G1 + 2)], s, s) for s in group_starts(count - 2)
    ]
    first_layer(groups, one_ref, bias_ref, comp3, hid3)
    blocks = [(s, EDGE + s) for s in range(0, TH - 2 * EDGE, 2 * G2)]
    second_layer(blocks, two_ref, bias_ref, hid3, out, out_ref, sems)


def outer_kernel(
    comp_ref, near_ref, far_ref, one_ref, two_ref, bias_ref, inner_ref, out_ref, beside, comp3, hid3, out, sems
):
    del inner_ref
    row_at = lax.axis_index("row")
    odd = row_at % 2
    beside[1 - odd] = near_ref[...]
    beside[odd] = far_ref[...]
    above, below = beside.at[0], beside.at[1]
    upper = [(above, 0), (above, 1)] + [(comp_ref, i) for i in range(EDGE + 2)]
    lower = [(comp_ref, TH - EDGE - 2 + i) for i in range(EDGE + 2)] + [(below, 0), (below, 1)]
    for i, (ref, row) in enumerate(upper + lower):
        shifted(ref, row, comp3, i)
    groups = []
    for part, rows in enumerate((upper, lower)):
        for s in group_starts(EDGE + 2):
            groups.append((rows[s : s + G1 + 2], part * (EDGE + 4) + s, part * (EDGE + 2) + s))
    first_layer(groups, one_ref, bias_ref, comp3, hid3)

    @pl.when(row_at == 0)
    def _():
        hid3[0] = jnp.zeros((3 * C, TW), BF)

    @pl.when(row_at == lax.axis_size("row") - 1)
    def _():
        hid3[2 * EDGE + 3] = jnp.zeros((3 * C, TW), BF)

    second_layer([(0, 0), (EDGE + 2, TH - EDGE)], two_ref, bias_ref, hid3, out, out_ref, sems)


def layer_scratch(rows, parts):
    return [
        pltpu.VMEM((rows + 4 * parts, 3 * FS, TW), BF),
        pltpu.VMEM((rows + 2 * parts, 3 * C, TW), BF),
        pltpu.VMEM((C, rows, TW), BF),
        pltpu.SemaphoreType.DMA((rows // (2 * G2),)),
    ]


def inner(comp, band1, band2, bias):
    rows = TH - 2 * EDGE
    return pl.pallas_call(
        inner_kernel,
        out_specs=pl.BlockSpec(memory_space=pl.ANY),
        out_shape=jax.ShapeDtypeStruct((C, TH, TW), BF),
        scratch_shapes=layer_scratch(rows, 1),
        compiler_params=pltpu.CompilerParams(vmem_limit_bytes=32 << 20),
        cost_estimate=pl.CostEstimate(
            flops=2 * (M1 * K1 + M2 * K2) * TW * 13, bytes_accessed=8_000_000, transcendentals=0
        ),
        name="inner",
    )(comp, band1, band2, bias)


def outer(comp, near, far, band1, band2, bias, inner_rows):
    vmem = pl.BlockSpec(memory_space=pltpu.VMEM)
    return pl.pallas_call(
        outer_kernel,
        in_specs=[vmem] * 6 + [pl.BlockSpec(memory_space=pl.ANY)],
        out_specs=pl.BlockSpec(memory_space=pl.ANY),
        out_shape=jax.ShapeDtypeStruct((C, TH, TW), BF),
        input_output_aliases={6: 0},
        scratch_shapes=[pltpu.VMEM((2, 2, FS, TW + LANES), BF)] + layer_scratch(2 * EDGE, 2),
        compiler_params=pltpu.CompilerParams(vmem_limit_bytes=32 << 20),
        name="outer",
    )(comp, near, far, band1, band2, bias, inner_rows)


def swap(x, axis, first):
    pairs = [(i, i + 1) for i in range(first, lax.axis_size(axis) - 1, 2)]
    return lax.ppermute(x, axis, pairs + [(j, i) for i, j in pairs])


def on_device(
    ray_rows,
    targets,
    cell_block,
    interp_weights,
    first_kernel,
    first_bias,
    second_kernel,
    second_bias,
):
    outgoing, band1, band2, bias = send(
        targets.T,
        cell_block.T,
        ray_rows.transpose(1, 0, 2),
        interp_weights,
        first_kernel.transpose(0, 2, 1),
        second_kernel,
        first_bias.reshape(1, C),
        second_bias.reshape(1, C),
    )
    incoming = lax.all_to_all(outgoing, ("row", "col"), split_axis=0, concat_axis=0, tiled=True)
    comp, near, far = receive(incoming)
    near = swap(near, "row", 0)
    far = swap(far, "row", 1)
    inner_rows = inner(comp, band1, band2, bias)
    return outer(comp, near, far, band1, band2, bias, inner_rows)


def solution(mesh):
    in_specs = (
        P(("row", "col"), None, None),
        P(("row", "col"), None),
        P(("row", "col"), None),
        P(("row", "col"), None, None, None),
        P(),
        P(),
        P(),
        P(),
    )
    out_specs = P(None, "row", "col")
    return jax.shard_map(
        on_device, mesh=mesh, in_specs=in_specs, out_specs=out_specs, check_vma=False
    )
```

```python
import jax
import jax.numpy as jnp
from jax import lax
from jax.experimental import pallas as pl
from jax.experimental.pallas import tpu as pltpu
from jax.sharding import PartitionSpec as P

F = 10
C = 32
LANES = 128
PIECES = 128
TILES = 128
TH = 128
TW = 256
CAP = 3
N_COL = 4
CHUNK = 16
OUT_PARTS = 4
FS = 16
SLAB = 40
PITCH = 24
RAYS = 136
G1 = 8
G2 = 8
EDGE = 2 * G2
RIGHT = 60
K1 = (G1 + 2) * 3 * FS
K2 = (G2 + 2) * 3 * C
M1 = G1 * C
M2 = G2 * C
BF = jnp.bfloat16
F32 = jnp.float32


def iota(shape, dim):
    return lax.broadcasted_iota(jnp.int32, shape, dim)


def one(mask):
    return jnp.where(mask, 1.0, 0.0).astype(BF)


def dot(a, b):
    return jnp.dot(a, b, preferred_element_type=F32)


def bands(first_ref, second_ref, bias_refs, one_ref, two_ref, bias_ref, taps, rows):
    taps[...] = jnp.zeros_like(taps)
    for tap in range(9):
        taps[tap * FS : tap * FS + F, 0:C] = first_ref[tap].astype(F32)
    first = taps[...].T[0:C, :]
    first = jnp.concatenate([first, jnp.zeros((C, 512 - 256), F32)], axis=1)
    for r in range(G1):
        moved = first if r == 0 else pltpu.roll(first, 3 * FS * r, 1)
        one_ref[r * C : (r + 1) * C, :] = moved[:, 0:K1].astype(BF)
    second = jnp.concatenate(
        [second_ref[tap].astype(F32) for tap in range(9)] + [jnp.zeros((C, 1024 - 9 * C), F32)], axis=1
    )
    for r in range(G2):
        moved = second if r == 0 else pltpu.roll(second, 3 * C * r, 1)
        for t in range(8):
            rows[t, pl.ds(r, C, stride=G2), :] = moved[:, t * LANES : (t + 1) * LANES]
    for t in range(8):
        width = min(LANES, K2 - t * LANES)
        two_ref[:, t * LANES : t * LANES + width] = rows[t, :, 0:width].astype(BF)
    for i, ref in enumerate(bias_refs):
        row = jnp.concatenate([ref[...], jnp.zeros((1, LANES - C), F32)], axis=1)
        bias_ref[i] = jnp.broadcast_to(row, (LANES, LANES)).T[0:C, :]


def send_kernel(
    tiles_hbm, blocks_hbm, ray_hbm, weights_ref, first_hbm, second_hbm, bias1_hbm, bias2_hbm,
    out_ref, one_hbm, two_hbm, bias_hbm,
    tiles_ref, blocks_ref, ray_ref, first_ref, second_ref, bias1_ref, bias2_ref,
    weights, rays, vals, columns, edges, slab, place, pick, out, taps, rows, one_ref, two_ref, bias_ref, sems
):
    steps = PIECES // CHUNK

    def arriving(i):
        chunk = pl.ds(pl.multiple_of(i * CHUNK, CHUNK), CHUNK)
        return pltpu.make_async_copy(weights_ref.at[chunk], weights.at[chunk], sems.at[i])

    def leaving(i):
        n = TILES // OUT_PARTS
        part = pl.ds(i * n, n)
        return pltpu.make_async_copy(out.at[part], out_ref.at[part], sems.at[steps + 10 + i])

    small = [
        pltpu.make_async_copy(source, target, sems.at[steps + i])
        for i, (source, target) in enumerate(
            (
                (tiles_hbm, tiles_ref),
                (blocks_hbm, blocks_ref),
                (ray_hbm, ray_ref),
                (first_hbm, first_ref),
                (second_hbm, second_ref),
                (bias1_hbm, bias1_ref),
                (bias2_hbm, bias2_ref),
                (one_ref, one_hbm),
                (two_ref, two_hbm),
                (bias_ref, bias_hbm),
            )
        )
    ]
    for copy in small[:7]:
        copy.start()
    for i in range(steps):
        arriving(i).start()

    def slots():
        tile = jnp.concatenate([tiles_ref[0:1, :], tiles_ref[1:2, :]], axis=1)
        block = jnp.concatenate([blocks_ref[0:1, :], blocks_ref[1:2, :]], axis=1)
        pairs = 2 * PIECES
        dest = iota((TILES, pairs), 0)
        mine = dest == tile
        before = one(iota((pairs, pairs), 0) < iota((pairs, pairs), 1))
        mine_f = jnp.where(mine, 1.0, 0.0)
        slot = jnp.sum(dot(mine_f.astype(BF), before) * mine_f, axis=0, keepdims=True)
        slot = slot.astype(jnp.int32)
        right_half = block % 2 == 1
        from_left = jnp.where(right_half, tile + 1, -1)
        from_left = jnp.where(from_left % N_COL == 0, -1, from_left)
        from_right = jnp.where(right_half | (tile % N_COL == 0), -1, tile - 1)
        for s in range(CAP):
            for kind, wanted in enumerate((tile, from_left, from_right)):
                wanted = jnp.where(slot == s, wanted, -1)
                at = (kind * CAP + s) * TILES
                place[at : at + TILES, :] = one(dest == wanted)
        lane = iota((1, LANES), 1)
        within = lane % 60
        frame = (within % 20) // 2
        wanted = frame * LANES + lane % 2 + jnp.where(lane < 60, LANES - 2, 0)
        wanted = jnp.where(lane < 120, wanted, -1)
        pick[...] = one(iota((F * LANES, LANES), 0) == wanted)
        spread = jnp.where(
            iota((LANES, pairs), 0) >= 120, jnp.broadcast_to(block.astype(F32), (LANES, pairs)), 0.0
        )
        edges[...] = spread.T

    small[0].wait()
    small[1].wait()
    slots()
    small[2].wait()
    for f in range(F):
        rays[f * RAYS : f * RAYS + PIECES, :] = ray_ref[f].astype(F32)

    for copy in small[3:7]:
        copy.wait()
    bands(first_ref, second_ref, (bias1_ref, bias2_ref), one_ref, two_ref, bias_ref, taps, rows)
    for copy in small[7:]:
        copy.start()

    @pl.loop(0, steps)
    def _(step):
        arriving(step).wait()
        for i in range(CHUNK):
            piece = step * CHUNK + i
            both = jnp.concatenate([weights[piece, 0], weights[piece, 1]], axis=1)
            ray = rays[pl.ds(piece, F, stride=RAYS), :].astype(BF)
            both = dot(ray, both)
            at = pl.multiple_of(piece * PITCH, 8)
            for k in range(2):
                vals[k, pl.ds(at, F), :] = both[:, k * LANES : (k + 1) * LANES]
        for k in range(2):
            to = pl.ds(pl.multiple_of(k * PIECES + step * CHUNK, CHUNK), CHUNK)
            for f in range(F):
                columns[to, f * LANES : (f + 1) * LANES] = vals[
                    k, pl.ds(step * CHUNK * PITCH + f, CHUNK, stride=PITCH), :
                ].astype(BF)

    def place_all():
        lane = iota((TILES, LANES), 1)
        for f2 in range(F // 2):
            moved = dot(place[0 : CAP * TILES, :], columns[:, 2 * f2 * LANES : (2 * f2 + 2) * LANES])
            for s in range(CAP):
                for half in range(2):
                    slab[pl.ds(s * F + 2 * f2 + half, TILES, stride=SLAB), :] = moved[
                        s * TILES : (s + 1) * TILES, half * LANES : (half + 1) * LANES
                    ]
        moved = dot(place[...], (edges[...] + dot(columns[...], pick[...])).astype(BF))
        own = jnp.zeros((TILES, LANES), F32)
        beside = jnp.zeros((TILES, LANES), F32)
        for s in range(CAP):
            own = jnp.where(lane == 120 + s, moved[s * TILES : (s + 1) * TILES], own)
            left = (lane // 20 == s) | (lane == 120 + s)
            at = (CAP + s) * TILES
            beside = jnp.where(left, moved[at : at + TILES], beside)
            right = (lane // 20 == CAP + s) | (lane == 123 + s)
            at = (2 * CAP + s) * TILES
            beside = jnp.where(right, moved[at : at + TILES], beside)
        slab[pl.ds(30, TILES, stride=SLAB), :] = own
        slab[pl.ds(31, TILES, stride=SLAB), :] = beside
        for i in range(OUT_PARTS):
            n = TILES // OUT_PARTS
            for d in range(i * n, (i + 1) * n):
                out[d] = slab[d * SLAB : d * SLAB + 32, :].astype(BF)
            leaving(i).start()
        for i in range(OUT_PARTS):
            leaving(i).wait()

    place_all()
    for copy in small[7:]:
        copy.wait()


def send(tiles, blocks, ray_rows, weights, first, second, bias1, bias2):
    pairs = 2 * PIECES
    return pl.pallas_call(
        send_kernel,
        in_specs=[pl.BlockSpec(memory_space=pl.ANY)] * 8,
        out_specs=[pl.BlockSpec(memory_space=pl.ANY)] * 4,
        out_shape=[
            jax.ShapeDtypeStruct((TILES, 32, LANES), BF),
            jax.ShapeDtypeStruct((M1, K1), BF),
            jax.ShapeDtypeStruct((M2, K2), BF),
            jax.ShapeDtypeStruct((2, C, LANES), F32),
        ],
        scratch_shapes=[
            pltpu.VMEM(tiles.shape, jnp.int32),
            pltpu.VMEM(blocks.shape, jnp.int32),
            pltpu.VMEM(ray_rows.shape, BF),
            pltpu.VMEM(first.shape, BF),
            pltpu.VMEM(second.shape, BF),
            pltpu.VMEM(bias1.shape, F32),
            pltpu.VMEM(bias2.shape, F32),
            pltpu.VMEM(weights.shape, BF),
            pltpu.VMEM((F * RAYS, LANES), F32),
            pltpu.VMEM((2, PIECES * PITCH, LANES), F32),
            pltpu.VMEM((pairs, F * LANES), BF),
            pltpu.VMEM((pairs, LANES), F32),
            pltpu.VMEM((TILES * SLAB, LANES), F32),
            pltpu.VMEM((3 * CAP * TILES, pairs), BF),
            pltpu.VMEM((F * LANES, LANES), BF),
            pltpu.VMEM((TILES, 32, LANES), BF),
            pltpu.VMEM((2 * LANES, LANES), F32),
            pltpu.VMEM((8, M2, LANES), F32),
            pltpu.VMEM((M1, K1), BF),
            pltpu.VMEM((M2, K2), BF),
            pltpu.VMEM((2, C, LANES), F32),
            pltpu.SemaphoreType.DMA((PIECES // CHUNK + 10 + OUT_PARTS,)),
        ],
        compiler_params=pltpu.CompilerParams(vmem_limit_bytes=58 << 20),
        name="send",
    )(tiles, blocks, ray_rows, weights, first, second, bias1, bias2)


def receive_kernel(in_ref, out_ref, near_ref, far_ref, slab, grid_f32, halo_f32):
    for d in range(TILES):
        slab[d * SLAB : d * SLAB + 32, :] = in_ref[d].astype(F32)
    own = slab[pl.ds(30, TILES, stride=SLAB), :].T
    beside = slab[pl.ds(31, TILES, stride=SLAB), :]
    beside_t = beside.T
    own_block = jnp.concatenate([own[120 + s : 121 + s, :] for s in range(CAP)], axis=1)
    own_block = own_block.astype(jnp.int32)
    at = (own_block % 2) * TH + own_block // 2
    spots = one(iota((2 * TH, CAP * TILES), 0) == at)
    zero = jnp.zeros((TH, LANES), F32)
    for f in range(F, FS):
        for half in range(2):
            grid_f32[half, pl.ds(f, TH, stride=PITCH), :] = zero
        halo_f32[pl.ds(f, TH, stride=PITCH), :] = zero
    lane = iota((TH, LANES), 1)
    edge_block = jnp.concatenate([beside_t[120 + s : 121 + s, :] for s in range(2 * CAP)], axis=1)
    edge_row = edge_block.astype(jnp.int32) // 2
    edge_spots = one(iota((TH, 2 * CAP * TILES), 0) == edge_row)
    edge_values = jnp.concatenate(
        [jnp.where(lane // 20 == s, beside, 0.0) for s in range(2 * CAP)], axis=0
    ).astype(BF)
    sides = dot(edge_spots, edge_values)
    sides = sides + pltpu.roll(sides, LANES - 20, 1) + pltpu.roll(sides, LANES - 40, 1)
    for f2 in range(F // 2):
        rhs = jnp.concatenate(
            [
                jnp.concatenate(
                    [slab[pl.ds(s * F + f, TILES, stride=SLAB), :].astype(BF) for s in range(CAP)],
                    axis=0,
                )
                for f in (2 * f2, 2 * f2 + 1)
            ],
            axis=1,
        )
        total = dot(spots, rhs)
        for i in range(2):
            f = 2 * f2 + i
            for half in range(2):
                grid_f32[half, pl.ds(f, TH, stride=PITCH), :] = total[
                    half * TH : (half + 1) * TH, i * LANES : (i + 1) * LANES
                ]
            halo = pltpu.roll(sides, LANES - 2 * f, 1) if f else sides
            halo_f32[pl.ds(f, TH, stride=PITCH), :] = halo
    for row in range(TH):
        rows = slice(row * PITCH, row * PITCH + FS)
        out_ref[row, :, 0:LANES] = grid_f32[0, rows, :].astype(BF)
        out_ref[row, :, LANES:TW] = grid_f32[1, rows, :].astype(BF)
        out_ref[row, :, TW : TW + LANES] = halo_f32[rows, :].astype(BF)

    odd = lax.axis_index("row") % 2 == 1

    @pl.when(odd)
    def _():
        near_ref[...] = out_ref[0:2]
        far_ref[...] = out_ref[TH - 2 : TH]

    @pl.when(jnp.logical_not(odd))
    def _():
        near_ref[...] = out_ref[TH - 2 : TH]
        far_ref[...] = out_ref[0:2]


def receive(incoming):
    return pl.pallas_call(
        receive_kernel,
        out_shape=[
            jax.ShapeDtypeStruct((TH, FS, TW + LANES), BF),
            jax.ShapeDtypeStruct((2, FS, TW + LANES), BF),
            jax.ShapeDtypeStruct((2, FS, TW + LANES), BF),
        ],
        scratch_shapes=[
            pltpu.VMEM((TILES * SLAB, LANES), F32),
            pltpu.VMEM((2, TH * PITCH, LANES), F32),
            pltpu.VMEM((TH * PITCH, LANES), F32),
        ],
        compiler_params=pltpu.CompilerParams(vmem_limit_bytes=24 << 20),
        name="receive",
    )(incoming)


def shifted(rows_ref, row, comp3, to):
    lane = iota((FS, LANES), 1)
    low = rows_ref[row, :, 0:LANES]
    high = rows_ref[row, :, LANES:TW]
    halo = rows_ref[row, :, TW : TW + LANES]
    low_up, high_up = pltpu.roll(low, 1, 1), pltpu.roll(high, 1, 1)
    comp3[to, 0:FS, 0:LANES] = jnp.where(lane == 0, pltpu.roll(halo, LANES - 1, 1), low_up)
    comp3[to, 0:FS, LANES:TW] = jnp.where(lane == 0, low_up, high_up)
    comp3[to, FS : 2 * FS, 0:LANES] = low
    comp3[to, FS : 2 * FS, LANES:TW] = high
    low_down, high_down = pltpu.roll(low, LANES - 1, 1), pltpu.roll(high, LANES - 1, 1)
    last = lane == LANES - 1
    comp3[to, 2 * FS : 3 * FS, 0:LANES] = jnp.where(last, high_down, low_down)
    comp3[to, 2 * FS : 3 * FS, LANES:TW] = jnp.where(
        last, pltpu.roll(halo, LANES - 1 - RIGHT, 1), high_down
    )


def first_layer_sides(groups, one_ref, bias):
    rows = (G1 + 2) * FS
    lane = iota((rows, LANES), 1)
    halos = jnp.zeros((rows, LANES), BF)
    firsts = jnp.zeros((rows, LANES), BF)
    lasts = jnp.zeros((rows, LANES), BF)
    for g, (window, _, _) in enumerate(groups):
        at = lambda lo, hi: jnp.concatenate([ref[i, :, lo:hi] for ref, i in window], axis=0)
        halo, low = at(TW, TW + LANES), at(0, LANES)
        if g:
            halo, low = pltpu.roll(halo, 2 * g, 1), pltpu.roll(low, 2 * g, 1)
        halos = jnp.where((lane // 2 == g) | (lane // 2 == RIGHT // 2 + g), halo, halos)
        firsts = jnp.where(lane == 2 * g, low, firsts)
        lasts = jnp.where(lane == RIGHT + 2 * g, pltpu.roll(at(LANES, TW), RIGHT + 1 + 2 * g, 1), lasts)
    halos_down = pltpu.roll(halos, LANES - 1, 1)
    packed = (
        jnp.where(lane < RIGHT, halos, lasts),
        jnp.where(lane < RIGHT, halos_down, halos),
        jnp.where(lane < RIGHT, firsts, halos_down),
    )
    packed = jnp.concatenate(
        [packed[dx][r * FS : (r + 1) * FS] for r in range(G1 + 2) for dx in range(3)], axis=0
    )
    side = dot(one_ref[...], packed).reshape(G1, C, LANES) + bias[None]
    side = jnp.maximum(side, 0.0)
    col_at = lax.axis_index("col")
    first_col = col_at == 0
    last_col = col_at == lax.axis_size("col") - 1
    lane = iota((G1, C, LANES), 2)
    side = jnp.where(((lane < RIGHT) & first_col) | ((lane >= RIGHT) & last_col), 0.0, side)
    return side.reshape(M1, LANES).astype(BF)


def first_layer(groups, one_ref, bias_ref, comp3, hid3):
    bias = bias_ref[0]
    wide_bias = jnp.concatenate([bias, bias], axis=1)[None]
    side = first_layer_sides(groups, one_ref, bias)
    lane = iota((M1, LANES), 1)
    first, last = lane == 0, lane == LANES - 1
    for g, (_, start, to) in enumerate(groups):
        window = comp3[start : start + G1 + 2].reshape(K1, TW)
        h = dot(one_ref[...], window).reshape(G1, C, TW) + wide_bias
        h = jnp.maximum(h, 0.0).reshape(M1, TW).astype(BF)
        low, high = h[:, 0:LANES], h[:, LANES:TW]
        low_up, high_up = pltpu.roll(low, 1, 1), pltpu.roll(high, 1, 1)
        low_down, high_down = pltpu.roll(low, LANES - 1, 1), pltpu.roll(high, LANES - 1, 1)
        left = pltpu.roll(side, LANES - 2 * g, 1) if g else side
        right = pltpu.roll(side, LANES - 1 - RIGHT - 2 * g, 1)
        tiles = (
            (jnp.where(first, left, low_up), jnp.where(first, low_up, high_up)),
            (low, high),
            (jnp.where(last, high_down, low_down), jnp.where(last, right, high_down)),
        )
        for dx in range(3):
            for t in range(2):
                hid3[to : to + G1, dx * C : (dx + 1) * C, t * LANES : (t + 1) * LANES] = tiles[dx][
                    t
                ].reshape(G1, C, LANES)


def second_layer(blocks, two_ref, bias_ref, hid3, out, out_ref, sems):
    bias = jnp.broadcast_to(bias_ref[1][:, None, :], (C, G2, LANES))
    bias = jnp.concatenate([bias, bias], axis=2)
    copies = []
    for i, (start, row) in enumerate(blocks):
        halves = []
        for half in range(2):
            at = start + half * G2
            x = dot(two_ref[...], hid3[at : at + G2 + 2].reshape(K2, TW))
            halves.append(jnp.maximum(x.reshape(C, G2, TW) + bias, 0.0))
        part = out.at[:, i * 2 * G2 : (i + 1) * 2 * G2, :]
        part[...] = jnp.concatenate(halves, axis=1).astype(BF)
        copy = pltpu.make_async_copy(part, out_ref.at[:, row : row + 2 * G2, :], sems.at[i])
        copy.start()
        copies.append(copy)
    for copy in copies:
        copy.wait()


def group_starts(count):
    return [*range(0, count - G1, G1), count - G1]


def inner_kernel(comp_ref, one_ref, two_ref, bias_ref, out_ref, comp3, hid3, out, sems):
    top, count = EDGE - 2, TH - 2 * EDGE + 4
    for i in range(count):
        shifted(comp_ref, top + i, comp3, i)
    groups = [
        ([(comp_ref, top + s + i) for i in range(G1 + 2)], s, s) for s in group_starts(count - 2)
    ]
    first_layer(groups, one_ref, bias_ref, comp3, hid3)
    blocks = [(s, EDGE + s) for s in range(0, TH - 2 * EDGE, 2 * G2)]
    second_layer(blocks, two_ref, bias_ref, hid3, out, out_ref, sems)


def outer_kernel(
    comp_ref, near_ref, far_ref, one_ref, two_ref, bias_ref, inner_ref, out_ref, beside, comp3, hid3, out, sems
):
    del inner_ref
    row_at = lax.axis_index("row")
    odd = row_at % 2
    beside[1 - odd] = near_ref[...]
    beside[odd] = far_ref[...]
    above, below = beside.at[0], beside.at[1]
    upper = [(above, 0), (above, 1)] + [(comp_ref, i) for i in range(EDGE + 2)]
    lower = [(comp_ref, TH - EDGE - 2 + i) for i in range(EDGE + 2)] + [(below, 0), (below, 1)]
    for i, (ref, row) in enumerate(upper + lower):
        shifted(ref, row, comp3, i)
    groups = []
    for part, rows in enumerate((upper, lower)):
        for s in group_starts(EDGE + 2):
            groups.append((rows[s : s + G1 + 2], part * (EDGE + 4) + s, part * (EDGE + 2) + s))
    first_layer(groups, one_ref, bias_ref, comp3, hid3)
    for row, outside in ((0, row_at == 0), (2 * EDGE + 3, row_at == lax.axis_size("row") - 1)):
        x = hid3[row]
        hid3[row] = jnp.where(outside, jnp.zeros_like(x), x)
    second_layer([(0, 0), (EDGE + 2, TH - EDGE)], two_ref, bias_ref, hid3, out, out_ref, sems)


def layer_scratch(rows, parts):
    return [
        pltpu.VMEM((rows + 4 * parts, 3 * FS, TW), BF),
        pltpu.VMEM((rows + 2 * parts, 3 * C, TW), BF),
        pltpu.VMEM((C, rows, TW), BF),
        pltpu.SemaphoreType.DMA((rows // (2 * G2),)),
    ]


def inner(comp, band1, band2, bias):
    rows = TH - 2 * EDGE
    return pl.pallas_call(
        inner_kernel,
        out_specs=pl.BlockSpec(memory_space=pl.ANY),
        out_shape=jax.ShapeDtypeStruct((C, TH, TW), BF),
        scratch_shapes=layer_scratch(rows, 1),
        compiler_params=pltpu.CompilerParams(vmem_limit_bytes=32 << 20),
        cost_estimate=pl.CostEstimate(
            flops=2 * (M1 * K1 + M2 * K2) * TW * 13, bytes_accessed=8_000_000, transcendentals=0
        ),
        name="inner",
    )(comp, band1, band2, bias)


def outer(comp, near, far, band1, band2, bias, inner_rows):
    vmem = pl.BlockSpec(memory_space=pltpu.VMEM)
    return pl.pallas_call(
        outer_kernel,
        in_specs=[vmem] * 6 + [pl.BlockSpec(memory_space=pl.ANY)],
        out_specs=pl.BlockSpec(memory_space=pl.ANY),
        out_shape=jax.ShapeDtypeStruct((C, TH, TW), BF),
        input_output_aliases={6: 0},
        scratch_shapes=[pltpu.VMEM((2, 2, FS, TW + LANES), BF)] + layer_scratch(2 * EDGE, 2),
        compiler_params=pltpu.CompilerParams(vmem_limit_bytes=32 << 20),
        name="outer",
    )(comp, near, far, band1, band2, bias, inner_rows)


def swap(x, axis, first):
    pairs = [(i, i + 1) for i in range(first, lax.axis_size(axis) - 1, 2)]
    return lax.ppermute(x, axis, pairs + [(j, i) for i, j in pairs])


def on_device(
    ray_rows,
    targets,
    cell_block,
    interp_weights,
    first_kernel,
    first_bias,
    second_kernel,
    second_bias,
):
    outgoing, band1, band2, bias = send(
        targets.T,
        cell_block.T,
        ray_rows.transpose(1, 0, 2),
        interp_weights,
        first_kernel.transpose(0, 2, 1),
        second_kernel,
        first_bias.reshape(1, C),
        second_bias.reshape(1, C),
    )
    incoming = lax.all_to_all(outgoing, ("row", "col"), split_axis=0, concat_axis=0, tiled=True)
    comp, near, far = receive(incoming)
    near = swap(near, "row", 0)
    far = swap(far, "row", 1)
    inner_rows = inner(comp, band1, band2, bias)
    return outer(comp, near, far, band1, band2, bias, inner_rows)


def solution(mesh):
    in_specs = (
        P(("row", "col"), None, None),
        P(("row", "col"), None),
        P(("row", "col"), None),
        P(("row", "col"), None, None, None),
        P(),
        P(),
        P(),
        P(),
    )
    out_specs = P(None, "row", "col")
    return jax.shard_map(
        on_device, mesh=mesh, in_specs=in_specs, out_specs=out_specs, check_vma=False
    )
```

```python
import jax
import jax.numpy as jnp
from jax import lax
from jax.experimental import pallas as pl
from jax.experimental.pallas import tpu as pltpu
from jax.sharding import PartitionSpec as P

F = 10
C = 32
LANES = 128
PIECES = 128
TILES = 128
TH = 128
TW = 256
CAP = 3
N_COL = 4
CHUNK = 16
OUT_PARTS = 2
EDGE_STEPS = (3, 6, 7)
FS = 16
SLAB = 40
PITCH = 24
RAYS = 136
G1 = 8
G2 = 8
EDGE = 2 * G2
RIGHT = 60
K1 = (G1 + 2) * 3 * FS
K2 = (G2 + 2) * 3 * C
M1 = G1 * C
M2 = G2 * C
BF = jnp.bfloat16
F32 = jnp.float32


def iota(shape, dim):
    return lax.broadcasted_iota(jnp.int32, shape, dim)


def one(mask):
    return jnp.where(mask, 1.0, 0.0).astype(BF)


def dot(a, b):
    return jnp.dot(a, b, preferred_element_type=F32)


def bands(first_ref, second_ref, bias_refs, one_ref, two_ref, bias_ref, taps, rows):
    taps[...] = jnp.zeros_like(taps)
    for tap in range(9):
        taps[tap * FS : tap * FS + F, 0:C] = first_ref[tap].astype(F32)
    first = taps[...].T[0:C, :]
    first = jnp.concatenate([first, jnp.zeros((C, 512 - 256), F32)], axis=1)
    for r in range(G1):
        moved = first if r == 0 else pltpu.roll(first, 3 * FS * r, 1)
        one_ref[r * C : (r + 1) * C, :] = moved[:, 0:K1].astype(BF)
    second = jnp.concatenate(
        [second_ref[tap].astype(F32) for tap in range(9)] + [jnp.zeros((C, 1024 - 9 * C), F32)], axis=1
    )
    for r in range(G2):
        moved = second if r == 0 else pltpu.roll(second, 3 * C * r, 1)
        for t in range(8):
            rows[t, pl.ds(r, C, stride=G2), :] = moved[:, t * LANES : (t + 1) * LANES]
    for t in range(8):
        width = min(LANES, K2 - t * LANES)
        two_ref[:, t * LANES : t * LANES + width] = rows[t, :, 0:width].astype(BF)
    for i, ref in enumerate(bias_refs):
        row = jnp.concatenate([ref[...], jnp.zeros((1, LANES - C), F32)], axis=1)
        bias_ref[i] = jnp.broadcast_to(row, (LANES, LANES)).T[0:C, :]


def send_kernel(
    tiles_hbm, blocks_hbm, ray_hbm, weights_ref, first_hbm, second_hbm, bias1_hbm, bias2_hbm,
    out_ref, one_hbm, two_hbm, bias_hbm,
    tiles_ref, blocks_ref, ray_ref, first_ref, second_ref, bias1_ref, bias2_ref,
    weights, rays, vals, columns, edges, slab, place, pick, out, taps, rows, one_ref, two_ref, bias_ref, sems
):
    steps = PIECES // CHUNK

    def arriving(i):
        chunk = pl.ds(pl.multiple_of(i * CHUNK, CHUNK), CHUNK)
        return pltpu.make_async_copy(weights_ref.at[chunk], weights.at[chunk], sems.at[i])

    def leaving(i):
        rows = pl.ds(16 * i, 16)
        return pltpu.make_async_copy(out.at[:, rows, :], out_ref.at[:, rows, :], sems.at[steps + 10 + i])

    def pack(i):
        for d in range(TILES):
            at = d * SLAB + 16 * i
            out[d, 16 * i : 16 * i + 16, :] = slab[at : at + 16, :].astype(BF)
        leaving(i).start()

    small = [
        pltpu.make_async_copy(source, target, sems.at[steps + i])
        for i, (source, target) in enumerate(
            (
                (tiles_hbm, tiles_ref),
                (blocks_hbm, blocks_ref),
                (ray_hbm, ray_ref),
                (first_hbm, first_ref),
                (second_hbm, second_ref),
                (bias1_hbm, bias1_ref),
                (bias2_hbm, bias2_ref),
                (one_ref, one_hbm),
                (two_ref, two_hbm),
                (bias_ref, bias_hbm),
            )
        )
    ]
    for copy in small[:7]:
        copy.start()
    for i in range(steps):
        arriving(i).start()

    def slots():
        tile = jnp.concatenate([tiles_ref[0:1, :], tiles_ref[1:2, :]], axis=1)
        block = jnp.concatenate([blocks_ref[0:1, :], blocks_ref[1:2, :]], axis=1)
        pairs = 2 * PIECES
        dest = iota((TILES, pairs), 0)
        mine = dest == tile
        before = one(iota((pairs, pairs), 0) < iota((pairs, pairs), 1))
        mine_f = jnp.where(mine, 1.0, 0.0)
        slot = jnp.sum(dot(mine_f.astype(BF), before) * mine_f, axis=0, keepdims=True)
        slot = slot.astype(jnp.int32)
        right_half = block % 2 == 1
        from_left = jnp.where(right_half, tile + 1, -1)
        from_left = jnp.where(from_left % N_COL == 0, -1, from_left)
        from_right = jnp.where(right_half | (tile % N_COL == 0), -1, tile - 1)
        for s in range(CAP):
            for kind, wanted in enumerate((tile, from_left, from_right)):
                wanted = jnp.where(slot == s, wanted, -1)
                at = (kind * CAP + s) * TILES
                place[at : at + TILES, :] = one(dest == wanted)
        lane = iota((1, LANES), 1)
        within = lane % 60
        frame = (within % 20) // 2
        wanted = frame * LANES + lane % 2 + jnp.where(lane < 60, LANES - 2, 0)
        wanted = jnp.where(lane < 120, wanted, -1)
        pick[...] = one(iota((F * LANES, LANES), 0) == wanted)
        spread = jnp.where(
            iota((LANES, pairs), 0) >= 120, jnp.broadcast_to(block.astype(F32), (LANES, pairs)), 0.0
        )
        edges[...] = spread.T

    small[0].wait()
    small[1].wait()
    slots()
    small[2].wait()
    for f in range(F):
        rays[f * RAYS : f * RAYS + PIECES, :] = ray_ref[f].astype(F32)

    for copy in small[3:7]:
        copy.wait()
    bands(first_ref, second_ref, (bias1_ref, bias2_ref), one_ref, two_ref, bias_ref, taps, rows)
    for copy in small[7:]:
        copy.start()

    done = 0
    for step in range(steps):
        arriving(step).wait()
        for i in range(CHUNK):
            piece = step * CHUNK + i
            both = jnp.concatenate([weights[piece, 0], weights[piece, 1]], axis=1)
            ray = rays[pl.ds(piece, F, stride=RAYS), :].astype(BF)
            both = dot(ray, both)
            at = pl.multiple_of(piece * PITCH, 8)
            for k in range(2):
                vals[k, pl.ds(at, F), :] = both[:, k * LANES : (k + 1) * LANES]
        for k in range(2):
            to = pl.ds(pl.multiple_of(k * PIECES + step * CHUNK, CHUNK), CHUNK)
            for f in range(F):
                columns[to, f * LANES : (f + 1) * LANES] = vals[
                    k, pl.ds(step * CHUNK * PITCH + f, CHUNK, stride=PITCH), :
                ].astype(BF)
        if step in EDGE_STEPS:
            pieces = slice(done, (step + 1) * CHUNK)
            both = jnp.concatenate([columns[pieces, :], columns[PIECES:, :][pieces]], axis=0)
            both = dot(both, pick[...])
            count = both.shape[0] // 2
            for k in range(2):
                at = k * PIECES + done
                edges[at : at + count, :] += both[k * count : (k + 1) * count]
            done = (step + 1) * CHUNK

    def place_all():
        lane = iota((TILES, LANES), 1)
        for f2 in range(F // 2):
            moved = dot(place[0 : CAP * TILES, :], columns[:, 2 * f2 * LANES : (2 * f2 + 2) * LANES])
            for s in range(CAP):
                for half in range(2):
                    slab[pl.ds(s * F + 2 * f2 + half, TILES, stride=SLAB), :] = moved[
                        s * TILES : (s + 1) * TILES, half * LANES : (half + 1) * LANES
                    ]
        pack(0)
        moved = dot(place[...], edges[...].astype(BF))
        own = jnp.zeros((TILES, LANES), F32)
        beside = jnp.zeros((TILES, LANES), F32)
        for s in range(CAP):
            own = jnp.where(lane == 120 + s, moved[s * TILES : (s + 1) * TILES], own)
            left = (lane // 20 == s) | (lane == 120 + s)
            at = (CAP + s) * TILES
            beside = jnp.where(left, moved[at : at + TILES], beside)
            right = (lane // 20 == CAP + s) | (lane == 123 + s)
            at = (2 * CAP + s) * TILES
            beside = jnp.where(right, moved[at : at + TILES], beside)
        slab[pl.ds(30, TILES, stride=SLAB), :] = own
        slab[pl.ds(31, TILES, stride=SLAB), :] = beside
        pack(1)
        for i in range(2):
            leaving(i).wait()

    place_all()
    for copy in small[7:]:
        copy.wait()


def send(tiles, blocks, ray_rows, weights, first, second, bias1, bias2):
    pairs = 2 * PIECES
    return pl.pallas_call(
        send_kernel,
        in_specs=[pl.BlockSpec(memory_space=pl.ANY)] * 8,
        out_specs=[pl.BlockSpec(memory_space=pl.ANY)] * 4,
        out_shape=[
            jax.ShapeDtypeStruct((TILES, 32, LANES), BF),
            jax.ShapeDtypeStruct((M1, K1), BF),
            jax.ShapeDtypeStruct((M2, K2), BF),
            jax.ShapeDtypeStruct((2, C, LANES), F32),
        ],
        scratch_shapes=[
            pltpu.VMEM(tiles.shape, jnp.int32),
            pltpu.VMEM(blocks.shape, jnp.int32),
            pltpu.VMEM(ray_rows.shape, BF),
            pltpu.VMEM(first.shape, BF),
            pltpu.VMEM(second.shape, BF),
            pltpu.VMEM(bias1.shape, F32),
            pltpu.VMEM(bias2.shape, F32),
            pltpu.VMEM(weights.shape, BF),
            pltpu.VMEM((FS * RAYS, LANES), F32),
            pltpu.VMEM((2, PIECES * PITCH, LANES), F32),
            pltpu.VMEM((pairs, F * LANES), BF),
            pltpu.VMEM((pairs, LANES), F32),
            pltpu.VMEM((TILES * SLAB, LANES), F32),
            pltpu.VMEM((3 * CAP * TILES, pairs), BF),
            pltpu.VMEM((F * LANES, LANES), BF),
            pltpu.VMEM((TILES, 32, LANES), BF),
            pltpu.VMEM((2 * LANES, LANES), F32),
            pltpu.VMEM((8, M2, LANES), F32),
            pltpu.VMEM((M1, K1), BF),
            pltpu.VMEM((M2, K2), BF),
            pltpu.VMEM((2, C, LANES), F32),
            pltpu.SemaphoreType.DMA((PIECES // CHUNK + 10 + OUT_PARTS,)),
        ],
        compiler_params=pltpu.CompilerParams(vmem_limit_bytes=58 << 20),
        name="send",
    )(tiles, blocks, ray_rows, weights, first, second, bias1, bias2)


def receive_kernel(in_ref, out_ref, near_ref, far_ref, slab, grid_f32, halo_f32):
    for d in range(TILES):
        slab[d * SLAB : d * SLAB + 32, :] = in_ref[d].astype(F32)
    own = slab[pl.ds(30, TILES, stride=SLAB), :].T
    beside = slab[pl.ds(31, TILES, stride=SLAB), :]
    beside_t = beside.T
    own_block = jnp.concatenate([own[120 + s : 121 + s, :] for s in range(CAP)], axis=1)
    own_block = own_block.astype(jnp.int32)
    at = (own_block % 2) * TH + own_block // 2
    spots = one(iota((2 * TH, CAP * TILES), 0) == at)
    lane = iota((TH, LANES), 1)
    edge_block = jnp.concatenate([beside_t[120 + s : 121 + s, :] for s in range(2 * CAP)], axis=1)
    edge_row = edge_block.astype(jnp.int32) // 2
    edge_spots = one(iota((TH, 2 * CAP * TILES), 0) == edge_row)
    edge_values = jnp.concatenate(
        [jnp.where(lane // 20 == s, beside, 0.0) for s in range(2 * CAP)], axis=0
    ).astype(BF)
    sides = dot(edge_spots, edge_values)
    sides = sides + pltpu.roll(sides, LANES - 20, 1) + pltpu.roll(sides, LANES - 40, 1)
    for f2 in range(F // 2):
        rhs = jnp.concatenate(
            [
                jnp.concatenate(
                    [slab[pl.ds(s * F + f, TILES, stride=SLAB), :].astype(BF) for s in range(CAP)],
                    axis=0,
                )
                for f in (2 * f2, 2 * f2 + 1)
            ],
            axis=1,
        )
        total = dot(spots, rhs)
        for i in range(2):
            f = 2 * f2 + i
            for half in range(2):
                grid_f32[half, pl.ds(f, TH, stride=PITCH), :] = total[
                    half * TH : (half + 1) * TH, i * LANES : (i + 1) * LANES
                ]
            halo = pltpu.roll(sides, LANES - 2 * f, 1) if f else sides
            halo_f32[pl.ds(f, TH, stride=PITCH), :] = halo
    frames = iota((FS, LANES), 0) < F
    for row in range(TH):
        rows = slice(row * PITCH, row * PITCH + FS)
        out_ref[row, :, 0:LANES] = jnp.where(frames, grid_f32[0, rows, :], 0.0).astype(BF)
        out_ref[row, :, LANES:TW] = jnp.where(frames, grid_f32[1, rows, :], 0.0).astype(BF)
        out_ref[row, :, TW : TW + LANES] = jnp.where(frames, halo_f32[rows, :], 0.0).astype(BF)

    odd = lax.axis_index("row") % 2 == 1

    @pl.when(odd)
    def _():
        near_ref[...] = out_ref[0:2]
        far_ref[...] = out_ref[TH - 2 : TH]

    @pl.when(jnp.logical_not(odd))
    def _():
        near_ref[...] = out_ref[TH - 2 : TH]
        far_ref[...] = out_ref[0:2]


def receive(incoming):
    return pl.pallas_call(
        receive_kernel,
        out_shape=[
            jax.ShapeDtypeStruct((TH, FS, TW + LANES), BF),
            jax.ShapeDtypeStruct((2, FS, TW + LANES), BF),
            jax.ShapeDtypeStruct((2, FS, TW + LANES), BF),
        ],
        scratch_shapes=[
            pltpu.VMEM((TILES * SLAB, LANES), F32),
            pltpu.VMEM((2, TH * PITCH, LANES), F32),
            pltpu.VMEM((TH * PITCH, LANES), F32),
        ],
        compiler_params=pltpu.CompilerParams(vmem_limit_bytes=24 << 20),
        name="receive",
    )(incoming)


def shifted(rows_ref, row, comp3, to):
    lane = iota((FS, LANES), 1)
    low = rows_ref[row, :, 0:LANES]
    high = rows_ref[row, :, LANES:TW]
    halo = rows_ref[row, :, TW : TW + LANES]
    low_up, high_up = pltpu.roll(low, 1, 1), pltpu.roll(high, 1, 1)
    comp3[to, 0:FS, 0:LANES] = jnp.where(lane == 0, pltpu.roll(halo, LANES - 1, 1), low_up)
    comp3[to, 0:FS, LANES:TW] = jnp.where(lane == 0, low_up, high_up)
    comp3[to, FS : 2 * FS, 0:LANES] = low
    comp3[to, FS : 2 * FS, LANES:TW] = high
    low_down, high_down = pltpu.roll(low, LANES - 1, 1), pltpu.roll(high, LANES - 1, 1)
    last = lane == LANES - 1
    comp3[to, 2 * FS : 3 * FS, 0:LANES] = jnp.where(last, high_down, low_down)
    comp3[to, 2 * FS : 3 * FS, LANES:TW] = jnp.where(
        last, pltpu.roll(halo, LANES - 1 - RIGHT, 1), high_down
    )


def first_layer_sides(groups, one_ref, bias):
    rows = (G1 + 2) * FS
    lane = iota((rows, LANES), 1)
    halos = jnp.zeros((rows, LANES), BF)
    firsts = jnp.zeros((rows, LANES), BF)
    lasts = jnp.zeros((rows, LANES), BF)
    for g, (window, _, _) in enumerate(groups):
        at = lambda lo, hi: jnp.concatenate([ref[i, :, lo:hi] for ref, i in window], axis=0)
        halo, low = at(TW, TW + LANES), at(0, LANES)
        if g:
            halo, low = pltpu.roll(halo, 2 * g, 1), pltpu.roll(low, 2 * g, 1)
        halos = jnp.where((lane // 2 == g) | (lane // 2 == RIGHT // 2 + g), halo, halos)
        firsts = jnp.where(lane == 2 * g, low, firsts)
        lasts = jnp.where(lane == RIGHT + 2 * g, pltpu.roll(at(LANES, TW), RIGHT + 1 + 2 * g, 1), lasts)
    halos_down = pltpu.roll(halos, LANES - 1, 1)
    packed = (
        jnp.where(lane < RIGHT, halos, lasts),
        jnp.where(lane < RIGHT, halos_down, halos),
        jnp.where(lane < RIGHT, firsts, halos_down),
    )
    packed = jnp.concatenate(
        [packed[dx][r * FS : (r + 1) * FS] for r in range(G1 + 2) for dx in range(3)], axis=0
    )
    side = dot(one_ref[...], packed).reshape(G1, C, LANES) + bias[None]
    side = jnp.maximum(side, 0.0)
    col_at = lax.axis_index("col")
    first_col = col_at == 0
    last_col = col_at == lax.axis_size("col") - 1
    lane = iota((G1, C, LANES), 2)
    side = jnp.where(((lane < RIGHT) & first_col) | ((lane >= RIGHT) & last_col), 0.0, side)
    return side.reshape(M1, LANES).astype(BF)


def first_layer(groups, one_ref, bias_ref, comp3, hid3):
    bias = bias_ref[0]
    wide_bias = jnp.concatenate([bias, bias], axis=1)[None]
    side = first_layer_sides(groups, one_ref, bias)
    lane = iota((M1, LANES), 1)
    first, last = lane == 0, lane == LANES - 1
    for g, (_, start, to) in enumerate(groups):
        window = comp3[start : start + G1 + 2].reshape(K1, TW)
        h = dot(one_ref[...], window).reshape(G1, C, TW) + wide_bias
        h = jnp.maximum(h, 0.0).reshape(M1, TW).astype(BF)
        low, high = h[:, 0:LANES], h[:, LANES:TW]
        low_up, high_up = pltpu.roll(low, 1, 1), pltpu.roll(high, 1, 1)
        low_down, high_down = pltpu.roll(low, LANES - 1, 1), pltpu.roll(high, LANES - 1, 1)
        left = pltpu.roll(side, LANES - 2 * g, 1) if g else side
        right = pltpu.roll(side, LANES - 1 - RIGHT - 2 * g, 1)
        tiles = (
            (jnp.where(first, left, low_up), jnp.where(first, low_up, high_up)),
            (low, high),
            (jnp.where(last, high_down, low_down), jnp.where(last, right, high_down)),
        )
        for dx in range(3):
            for t in range(2):
                hid3[to : to + G1, dx * C : (dx + 1) * C, t * LANES : (t + 1) * LANES] = tiles[dx][
                    t
                ].reshape(G1, C, LANES)


def second_layer(blocks, two_ref, bias_ref, hid3, out, out_ref, sems):
    bias = jnp.broadcast_to(bias_ref[1][:, None, :], (C, G2, LANES))
    bias = jnp.concatenate([bias, bias], axis=2)
    copies = []
    for i, (start, row) in enumerate(blocks):
        halves = []
        for half in range(2):
            at = start + half * G2
            x = dot(two_ref[...], hid3[at : at + G2 + 2].reshape(K2, TW))
            halves.append(jnp.maximum(x.reshape(C, G2, TW) + bias, 0.0))
        part = out.at[:, i * 2 * G2 : (i + 1) * 2 * G2, :]
        part[...] = jnp.concatenate(halves, axis=1).astype(BF)
        copy = pltpu.make_async_copy(part, out_ref.at[:, row : row + 2 * G2, :], sems.at[i])
        copy.start()
        copies.append(copy)
    for copy in copies:
        copy.wait()


def group_starts(count):
    return [*range(0, count - G1, G1), count - G1]


def inner_kernel(comp_ref, one_ref, two_ref, bias_ref, out_ref, comp3, hid3, out, sems):
    top, count = EDGE - 2, TH - 2 * EDGE + 4
    for i in range(count):
        shifted(comp_ref, top + i, comp3, i)
    groups = [
        ([(comp_ref, top + s + i) for i in range(G1 + 2)], s, s) for s in group_starts(count - 2)
    ]
    first_layer(groups, one_ref, bias_ref, comp3, hid3)
    blocks = [(s, EDGE + s) for s in range(0, TH - 2 * EDGE, 2 * G2)]
    second_layer(blocks, two_ref, bias_ref, hid3, out, out_ref, sems)


def outer_kernel(
    comp_ref, near_ref, far_ref, one_ref, two_ref, bias_ref, inner_ref, out_ref, beside, comp3, hid3, out, sems
):
    del inner_ref
    row_at = lax.axis_index("row")
    odd = row_at % 2
    beside[1 - odd] = near_ref[...]
    beside[odd] = far_ref[...]
    above, below = beside.at[0], beside.at[1]
    upper = [(above, 0), (above, 1)] + [(comp_ref, i) for i in range(EDGE + 2)]
    lower = [(comp_ref, TH - EDGE - 2 + i) for i in range(EDGE + 2)] + [(below, 0), (below, 1)]
    for i, (ref, row) in enumerate(upper + lower):
        shifted(ref, row, comp3, i)
    groups = []
    for part, rows in enumerate((upper, lower)):
        for s in group_starts(EDGE + 2):
            groups.append((rows[s : s + G1 + 2], part * (EDGE + 4) + s, part * (EDGE + 2) + s))
    first_layer(groups, one_ref, bias_ref, comp3, hid3)
    for row, outside in ((0, row_at == 0), (2 * EDGE + 3, row_at == lax.axis_size("row") - 1)):
        x = hid3[row]
        hid3[row] = jnp.where(outside, jnp.zeros_like(x), x)
    second_layer([(0, 0), (EDGE + 2, TH - EDGE)], two_ref, bias_ref, hid3, out, out_ref, sems)


def layer_scratch(rows, parts):
    return [
        pltpu.VMEM((rows + 4 * parts, 3 * FS, TW), BF),
        pltpu.VMEM((rows + 2 * parts, 3 * C, TW), BF),
        pltpu.VMEM((C, rows, TW), BF),
        pltpu.SemaphoreType.DMA((rows // (2 * G2),)),
    ]


def inner(comp, band1, band2, bias):
    rows = TH - 2 * EDGE
    return pl.pallas_call(
        inner_kernel,
        out_specs=pl.BlockSpec(memory_space=pl.ANY),
        out_shape=jax.ShapeDtypeStruct((C, TH, TW), BF),
        scratch_shapes=layer_scratch(rows, 1),
        compiler_params=pltpu.CompilerParams(vmem_limit_bytes=32 << 20),
        cost_estimate=pl.CostEstimate(
            flops=2 * (M1 * K1 + M2 * K2) * TW * 13, bytes_accessed=8_000_000, transcendentals=0
        ),
        name="inner",
    )(comp, band1, band2, bias)


def outer(comp, near, far, band1, band2, bias, inner_rows):
    vmem = pl.BlockSpec(memory_space=pltpu.VMEM)
    return pl.pallas_call(
        outer_kernel,
        in_specs=[vmem] * 6 + [pl.BlockSpec(memory_space=pl.ANY)],
        out_specs=pl.BlockSpec(memory_space=pl.ANY),
        out_shape=jax.ShapeDtypeStruct((C, TH, TW), BF),
        input_output_aliases={6: 0},
        scratch_shapes=[pltpu.VMEM((2, 2, FS, TW + LANES), BF)] + layer_scratch(2 * EDGE, 2),
        compiler_params=pltpu.CompilerParams(vmem_limit_bytes=32 << 20),
        name="outer",
    )(comp, near, far, band1, band2, bias, inner_rows)


def swap(x, axis, first):
    pairs = [(i, i + 1) for i in range(first, lax.axis_size(axis) - 1, 2)]
    return lax.ppermute(x, axis, pairs + [(j, i) for i, j in pairs])


def on_device(
    ray_rows,
    targets,
    cell_block,
    interp_weights,
    first_kernel,
    first_bias,
    second_kernel,
    second_bias,
):
    outgoing, band1, band2, bias = send(
        targets.T,
        cell_block.T,
        ray_rows.transpose(1, 0, 2),
        interp_weights,
        first_kernel.transpose(0, 2, 1),
        second_kernel,
        first_bias.reshape(1, C),
        second_bias.reshape(1, C),
    )
    incoming = lax.all_to_all(outgoing, ("row", "col"), split_axis=0, concat_axis=0, tiled=True)
    comp, near, far = receive(incoming)
    near = swap(near, "row", 0)
    far = swap(far, "row", 1)
    inner_rows = inner(comp, band1, band2, bias)
    return outer(comp, near, far, band1, band2, bias, inner_rows)


def solution(mesh):
    in_specs = (
        P(("row", "col"), None, None),
        P(("row", "col"), None),
        P(("row", "col"), None),
        P(("row", "col"), None, None, None),
        P(),
        P(),
        P(),
        P(),
    )
    out_specs = P(None, "row", "col")
    return jax.shard_map(
        on_device, mesh=mesh, in_specs=in_specs, out_specs=out_specs, check_vma=False
    )
```

```python
import jax
import jax.numpy as jnp
from jax import lax
from jax.experimental import pallas as pl
from jax.experimental.pallas import tpu as pltpu
from jax.sharding import PartitionSpec as P

F = 10
C = 32
LANES = 128
PIECES = 128
TILES = 128
TH = 128
TW = 256
CAP = 3
N_COL = 4
CHUNK = 16
OUT_PARTS = 2
EDGE_STEPS = (3, 6, 7)
FS = 16
SLAB = 36
PITCH = 24
RAYS = 136
G1 = 8
G2 = 8
EDGE = 2 * G2
RIGHT = 60
K1 = (G1 + 2) * 3 * FS
K2 = (G2 + 2) * 3 * C
M1 = G1 * C
M2 = G2 * C
BF = jnp.bfloat16
F32 = jnp.float32


def iota(shape, dim):
    return lax.broadcasted_iota(jnp.int32, shape, dim)


def one(mask):
    return jnp.where(mask, 1.0, 0.0).astype(BF)


def dot(a, b):
    return jnp.dot(a, b, preferred_element_type=F32)


def bands(first_ref, second_ref, bias_refs, one_ref, two_ref, bias_ref, taps, rows):
    taps[...] = jnp.zeros_like(taps)
    for tap in range(9):
        taps[tap * FS : tap * FS + F, 0:C] = first_ref[tap].astype(F32)
    first = taps[...].T[0:C, :]
    first = jnp.concatenate([first, jnp.zeros((C, 512 - 256), F32)], axis=1)
    for r in range(G1):
        moved = first if r == 0 else pltpu.roll(first, 3 * FS * r, 1)
        one_ref[r * C : (r + 1) * C, :] = moved[:, 0:K1].astype(BF)
    second = jnp.concatenate(
        [second_ref[tap].astype(F32) for tap in range(9)] + [jnp.zeros((C, 1024 - 9 * C), F32)], axis=1
    )
    for r in range(G2):
        moved = second if r == 0 else pltpu.roll(second, 3 * C * r, 1)
        for t in range(8):
            rows[t, pl.ds(r, C, stride=G2), :] = moved[:, t * LANES : (t + 1) * LANES]
    for t in range(8):
        width = min(LANES, K2 - t * LANES)
        two_ref[:, t * LANES : t * LANES + width] = rows[t, :, 0:width].astype(BF)
    for i, ref in enumerate(bias_refs):
        row = jnp.concatenate([ref[...], jnp.zeros((1, LANES - C), F32)], axis=1)
        bias_ref[i] = jnp.broadcast_to(row, (LANES, LANES)).T[0:C, :]


def send_kernel(
    tiles_hbm, blocks_hbm, ray_hbm, weights_ref, first_hbm, second_hbm, bias1_hbm, bias2_hbm,
    out_ref, one_hbm, two_hbm, bias_hbm,
    tiles_ref, blocks_ref, ray_ref, first_ref, second_ref, bias1_ref, bias2_ref,
    weights, rays, vals, columns, edges, slab, place, pick, out, taps, rows, one_ref, two_ref, bias_ref, sems
):
    steps = PIECES // CHUNK

    def arriving(i):
        chunk = pl.ds(pl.multiple_of(i * CHUNK, CHUNK), CHUNK)
        return pltpu.make_async_copy(weights_ref.at[chunk], weights.at[chunk], sems.at[i])

    def leaving(i):
        rows = pl.ds(16 * i, 16)
        return pltpu.make_async_copy(out.at[:, rows, :], out_ref.at[:, rows, :], sems.at[steps + 10 + i])

    def pack(i):
        for d in range(TILES):
            at = d * SLAB + 16 * i
            out[d, 16 * i : 16 * i + 16, :] = slab[at : at + 16, :].astype(BF)
        leaving(i).start()

    small = [
        pltpu.make_async_copy(source, target, sems.at[steps + i])
        for i, (source, target) in enumerate(
            (
                (tiles_hbm, tiles_ref),
                (blocks_hbm, blocks_ref),
                (ray_hbm, ray_ref),
                (first_hbm, first_ref),
                (second_hbm, second_ref),
                (bias1_hbm, bias1_ref),
                (bias2_hbm, bias2_ref),
                (one_ref, one_hbm),
                (two_ref, two_hbm),
                (bias_ref, bias_hbm),
            )
        )
    ]
    for copy in small[:7]:
        copy.start()
    for i in range(steps):
        arriving(i).start()

    def slots():
        tile = jnp.concatenate([tiles_ref[0:1, :], tiles_ref[1:2, :]], axis=1)
        block = jnp.concatenate([blocks_ref[0:1, :], blocks_ref[1:2, :]], axis=1)
        pairs = 2 * PIECES
        dest = iota((TILES, pairs), 0)
        mine = dest == tile
        before = one(iota((pairs, pairs), 0) < iota((pairs, pairs), 1))
        mine_f = jnp.where(mine, 1.0, 0.0)
        slot = jnp.sum(dot(mine_f.astype(BF), before) * mine_f, axis=0, keepdims=True)
        slot = slot.astype(jnp.int32)
        right_half = block % 2 == 1
        from_left = jnp.where(right_half, tile + 1, -1)
        from_left = jnp.where(from_left % N_COL == 0, -1, from_left)
        from_right = jnp.where(right_half | (tile % N_COL == 0), -1, tile - 1)
        for s in range(CAP):
            for kind, wanted in enumerate((tile, from_left, from_right)):
                wanted = jnp.where(slot == s, wanted, -1)
                at = (kind * CAP + s) * TILES
                place[at : at + TILES, :] = one(dest == wanted)
        lane = iota((1, LANES), 1)
        within = lane % 60
        frame = (within % 20) // 2
        wanted = frame * LANES + lane % 2 + jnp.where(lane < 60, LANES - 2, 0)
        wanted = jnp.where(lane < 120, wanted, -1)
        pick[...] = one(iota((F * LANES, LANES), 0) == wanted)
        spread = jnp.where(
            iota((LANES, pairs), 0) >= 120, jnp.broadcast_to(block.astype(F32), (LANES, pairs)), 0.0
        )
        edges[...] = spread.T

    small[0].wait()
    small[1].wait()
    slots()
    small[2].wait()
    for f in range(F):
        rays[f * RAYS : f * RAYS + PIECES, :] = ray_ref[f].astype(F32)

    for copy in small[3:7]:
        copy.wait()
    bands(first_ref, second_ref, (bias1_ref, bias2_ref), one_ref, two_ref, bias_ref, taps, rows)
    for copy in small[7:]:
        copy.start()

    done = 0
    for step in range(steps):
        arriving(step).wait()
        for i in range(CHUNK):
            piece = step * CHUNK + i
            both = jnp.concatenate([weights[piece, 0], weights[piece, 1]], axis=1)
            ray = rays[pl.ds(piece, F, stride=RAYS), :].astype(BF)
            both = dot(ray, both)
            at = pl.multiple_of(piece * PITCH, 8)
            for k in range(2):
                vals[k, pl.ds(at, F), :] = both[:, k * LANES : (k + 1) * LANES]
        for k in range(2):
            to = pl.ds(pl.multiple_of(k * PIECES + step * CHUNK, CHUNK), CHUNK)
            for f in range(F):
                columns[to, f * LANES : (f + 1) * LANES] = vals[
                    k, pl.ds(step * CHUNK * PITCH + f, CHUNK, stride=PITCH), :
                ].astype(BF)
        if step in EDGE_STEPS:
            pieces = slice(done, (step + 1) * CHUNK)
            both = jnp.concatenate([columns[pieces, :], columns[PIECES:, :][pieces]], axis=0)
            both = dot(both, pick[...])
            count = both.shape[0] // 2
            for k in range(2):
                at = k * PIECES + done
                edges[at : at + count, :] += both[k * count : (k + 1) * count]
            done = (step + 1) * CHUNK

    def place_all():
        lane = iota((TILES, LANES), 1)
        for f2 in range(F // 2):
            moved = dot(place[0 : CAP * TILES, :], columns[:, 2 * f2 * LANES : (2 * f2 + 2) * LANES])
            for s in range(CAP):
                for half in range(2):
                    slab[pl.ds(s * F + 2 * f2 + half, TILES, stride=SLAB), :] = moved[
                        s * TILES : (s + 1) * TILES, half * LANES : (half + 1) * LANES
                    ]
        pack(0)
        moved = dot(place[...], edges[...].astype(BF))
        own = jnp.zeros((TILES, LANES), F32)
        beside = jnp.zeros((TILES, LANES), F32)
        for s in range(CAP):
            own = jnp.where(lane == 120 + s, moved[s * TILES : (s + 1) * TILES], own)
            left = (lane // 20 == s) | (lane == 120 + s)
            at = (CAP + s) * TILES
            beside = jnp.where(left, moved[at : at + TILES], beside)
            right = (lane // 20 == CAP + s) | (lane == 123 + s)
            at = (2 * CAP + s) * TILES
            beside = jnp.where(right, moved[at : at + TILES], beside)
        slab[pl.ds(30, TILES, stride=SLAB), :] = own
        slab[pl.ds(31, TILES, stride=SLAB), :] = beside
        pack(1)
        for i in range(2):
            leaving(i).wait()

    place_all()
    for copy in small[7:]:
        copy.wait()


def send(tiles, blocks, ray_rows, weights, first, second, bias1, bias2):
    pairs = 2 * PIECES
    return pl.pallas_call(
        send_kernel,
        in_specs=[pl.BlockSpec(memory_space=pl.ANY)] * 8,
        out_specs=[pl.BlockSpec(memory_space=pl.ANY)] * 4,
        out_shape=[
            jax.ShapeDtypeStruct((TILES, 32, LANES), BF),
            jax.ShapeDtypeStruct((M1, K1), BF),
            jax.ShapeDtypeStruct((M2, K2), BF),
            jax.ShapeDtypeStruct((2, C, LANES), F32),
        ],
        scratch_shapes=[
            pltpu.VMEM(tiles.shape, jnp.int32),
            pltpu.VMEM(blocks.shape, jnp.int32),
            pltpu.VMEM(ray_rows.shape, BF),
            pltpu.VMEM(first.shape, BF),
            pltpu.VMEM(second.shape, BF),
            pltpu.VMEM(bias1.shape, F32),
            pltpu.VMEM(bias2.shape, F32),
            pltpu.VMEM(weights.shape, BF),
            pltpu.VMEM((FS * RAYS, LANES), F32),
            pltpu.VMEM((2, PIECES * PITCH, LANES), F32),
            pltpu.VMEM((pairs, F * LANES), BF),
            pltpu.VMEM((pairs, LANES), F32),
            pltpu.VMEM((TILES * SLAB, LANES), F32),
            pltpu.VMEM((3 * CAP * TILES, pairs), BF),
            pltpu.VMEM((F * LANES, LANES), BF),
            pltpu.VMEM((TILES, 32, LANES), BF),
            pltpu.VMEM((2 * LANES, LANES), F32),
            pltpu.VMEM((8, M2, LANES), F32),
            pltpu.VMEM((M1, K1), BF),
            pltpu.VMEM((M2, K2), BF),
            pltpu.VMEM((2, C, LANES), F32),
            pltpu.SemaphoreType.DMA((PIECES // CHUNK + 10 + OUT_PARTS,)),
        ],
        compiler_params=pltpu.CompilerParams(vmem_limit_bytes=58 << 20),
        name="send",
    )(tiles, blocks, ray_rows, weights, first, second, bias1, bias2)


def receive_kernel(in_ref, out_ref, near_ref, far_ref, slab, grid_f32, halo_f32):
    for d in range(TILES):
        slab[d * SLAB : d * SLAB + 32, :] = in_ref[d].astype(F32)
    own = slab[pl.ds(30, TILES, stride=SLAB), :].T
    beside = slab[pl.ds(31, TILES, stride=SLAB), :]
    beside_t = beside.T
    own_block = jnp.concatenate([own[120 + s : 121 + s, :] for s in range(CAP)], axis=1)
    own_block = own_block.astype(jnp.int32)
    at = (own_block % 2) * TH + own_block // 2
    spots = one(iota((2 * TH, CAP * TILES), 0) == at)
    lane = iota((TH, LANES), 1)
    edge_block = jnp.concatenate([beside_t[120 + s : 121 + s, :] for s in range(2 * CAP)], axis=1)
    edge_row = edge_block.astype(jnp.int32) // 2
    edge_spots = one(iota((TH, 2 * CAP * TILES), 0) == edge_row)
    edge_values = jnp.concatenate(
        [jnp.where(lane // 20 == s, beside, 0.0) for s in range(2 * CAP)], axis=0
    ).astype(BF)
    sides = dot(edge_spots, edge_values)
    sides = sides + pltpu.roll(sides, LANES - 20, 1) + pltpu.roll(sides, LANES - 40, 1)
    for f2 in range(F // 2):
        rhs = jnp.concatenate(
            [
                jnp.concatenate(
                    [slab[pl.ds(s * F + f, TILES, stride=SLAB), :].astype(BF) for s in range(CAP)],
                    axis=0,
                )
                for f in (2 * f2, 2 * f2 + 1)
            ],
            axis=1,
        )
        total = dot(spots, rhs)
        for i in range(2):
            f = 2 * f2 + i
            for half in range(2):
                grid_f32[half, pl.ds(f, TH, stride=PITCH), :] = total[
                    half * TH : (half + 1) * TH, i * LANES : (i + 1) * LANES
                ]
            halo = pltpu.roll(sides, LANES - 2 * f, 1) if f else sides
            halo_f32[pl.ds(f, TH, stride=PITCH), :] = halo
    frames = iota((FS, LANES), 0) < F
    for row in range(TH):
        rows = slice(row * PITCH, row * PITCH + FS)
        out_ref[row, :, 0:LANES] = jnp.where(frames, grid_f32[0, rows, :], 0.0).astype(BF)
        out_ref[row, :, LANES:TW] = jnp.where(frames, grid_f32[1, rows, :], 0.0).astype(BF)
        out_ref[row, :, TW : TW + LANES] = jnp.where(frames, halo_f32[rows, :], 0.0).astype(BF)

    odd = lax.axis_index("row") % 2 == 1

    @pl.when(odd)
    def _():
        near_ref[...] = out_ref[0:2]
        far_ref[...] = out_ref[TH - 2 : TH]

    @pl.when(jnp.logical_not(odd))
    def _():
        near_ref[...] = out_ref[TH - 2 : TH]
        far_ref[...] = out_ref[0:2]


def receive(incoming):
    return pl.pallas_call(
        receive_kernel,
        out_shape=[
            jax.ShapeDtypeStruct((TH, FS, TW + LANES), BF),
            jax.ShapeDtypeStruct((2, FS, TW + LANES), BF),
            jax.ShapeDtypeStruct((2, FS, TW + LANES), BF),
        ],
        scratch_shapes=[
            pltpu.VMEM((TILES * SLAB, LANES), F32),
            pltpu.VMEM((2, TH * PITCH, LANES), F32),
            pltpu.VMEM((TH * PITCH, LANES), F32),
        ],
        compiler_params=pltpu.CompilerParams(vmem_limit_bytes=24 << 20),
        name="receive",
    )(incoming)


def shifted(rows_ref, row, comp3, to):
    lane = iota((FS, LANES), 1)
    low = rows_ref[row, :, 0:LANES]
    high = rows_ref[row, :, LANES:TW]
    halo = rows_ref[row, :, TW : TW + LANES]
    low_up, high_up = pltpu.roll(low, 1, 1), pltpu.roll(high, 1, 1)
    comp3[to, 0:FS, 0:LANES] = jnp.where(lane == 0, pltpu.roll(halo, LANES - 1, 1), low_up)
    comp3[to, 0:FS, LANES:TW] = jnp.where(lane == 0, low_up, high_up)
    comp3[to, FS : 2 * FS, 0:LANES] = low
    comp3[to, FS : 2 * FS, LANES:TW] = high
    low_down, high_down = pltpu.roll(low, LANES - 1, 1), pltpu.roll(high, LANES - 1, 1)
    last = lane == LANES - 1
    comp3[to, 2 * FS : 3 * FS, 0:LANES] = jnp.where(last, high_down, low_down)
    comp3[to, 2 * FS : 3 * FS, LANES:TW] = jnp.where(
        last, pltpu.roll(halo, LANES - 1 - RIGHT, 1), high_down
    )


def first_layer_sides(groups, one_ref, bias):
    rows = (G1 + 2) * FS
    lane = iota((rows, LANES), 1)
    halos = jnp.zeros((rows, LANES), BF)
    firsts = jnp.zeros((rows, LANES), BF)
    lasts = jnp.zeros((rows, LANES), BF)
    for g, (window, _, _) in enumerate(groups):
        at = lambda lo, hi: jnp.concatenate([ref[i, :, lo:hi] for ref, i in window], axis=0)
        halo, low = at(TW, TW + LANES), at(0, LANES)
        if g:
            halo, low = pltpu.roll(halo, 2 * g, 1), pltpu.roll(low, 2 * g, 1)
        halos = jnp.where((lane // 2 == g) | (lane // 2 == RIGHT // 2 + g), halo, halos)
        firsts = jnp.where(lane == 2 * g, low, firsts)
        lasts = jnp.where(lane == RIGHT + 2 * g, pltpu.roll(at(LANES, TW), RIGHT + 1 + 2 * g, 1), lasts)
    halos_down = pltpu.roll(halos, LANES - 1, 1)
    packed = (
        jnp.where(lane < RIGHT, halos, lasts),
        jnp.where(lane < RIGHT, halos_down, halos),
        jnp.where(lane < RIGHT, firsts, halos_down),
    )
    packed = jnp.concatenate(
        [packed[dx][r * FS : (r + 1) * FS] for r in range(G1 + 2) for dx in range(3)], axis=0
    )
    side = dot(one_ref[...], packed).reshape(G1, C, LANES) + bias[None]
    side = jnp.maximum(side, 0.0)
    col_at = lax.axis_index("col")
    first_col = col_at == 0
    last_col = col_at == lax.axis_size("col") - 1
    lane = iota((G1, C, LANES), 2)
    side = jnp.where(((lane < RIGHT) & first_col) | ((lane >= RIGHT) & last_col), 0.0, side)
    return side.reshape(M1, LANES).astype(BF)


def first_layer(groups, one_ref, bias_ref, comp3, hid3):
    bias = bias_ref[0]
    wide_bias = jnp.concatenate([bias, bias], axis=1)[None]
    side = first_layer_sides(groups, one_ref, bias)
    lane = iota((M1, LANES), 1)
    first, last = lane == 0, lane == LANES - 1
    for g, (_, start, to) in enumerate(groups):
        window = comp3[start : start + G1 + 2].reshape(K1, TW)
        h = dot(one_ref[...], window).reshape(G1, C, TW) + wide_bias
        h = jnp.maximum(h, 0.0).reshape(M1, TW).astype(BF)
        low, high = h[:, 0:LANES], h[:, LANES:TW]
        low_up, high_up = pltpu.roll(low, 1, 1), pltpu.roll(high, 1, 1)
        low_down, high_down = pltpu.roll(low, LANES - 1, 1), pltpu.roll(high, LANES - 1, 1)
        left = pltpu.roll(side, LANES - 2 * g, 1) if g else side
        right = pltpu.roll(side, LANES - 1 - RIGHT - 2 * g, 1)
        tiles = (
            (jnp.where(first, left, low_up), jnp.where(first, low_up, high_up)),
            (low, high),
            (jnp.where(last, high_down, low_down), jnp.where(last, right, high_down)),
        )
        for dx in range(3):
            for t in range(2):
                hid3[to : to + G1, dx * C : (dx + 1) * C, t * LANES : (t + 1) * LANES] = tiles[dx][
                    t
                ].reshape(G1, C, LANES)


def second_layer(blocks, two_ref, bias_ref, hid3, out, out_ref, sems):
    bias = jnp.broadcast_to(bias_ref[1][:, None, :], (C, G2, LANES))
    bias = jnp.concatenate([bias, bias], axis=2)
    copies = []
    for i, (start, row) in enumerate(blocks):
        halves = []
        for half in range(2):
            at = start + half * G2
            x = dot(two_ref[...], hid3[at : at + G2 + 2].reshape(K2, TW))
            halves.append(jnp.maximum(x.reshape(C, G2, TW) + bias, 0.0))
        part = out.at[:, i * 2 * G2 : (i + 1) * 2 * G2, :]
        part[...] = jnp.concatenate(halves, axis=1).astype(BF)
        copy = pltpu.make_async_copy(part, out_ref.at[:, row : row + 2 * G2, :], sems.at[i])
        copy.start()
        copies.append(copy)
    for copy in copies:
        copy.wait()


def group_starts(count):
    return [*range(0, count - G1, G1), count - G1]


def inner_kernel(comp_ref, one_ref, two_ref, bias_ref, out_ref, comp3, hid3, out, sems):
    top, count = EDGE - 2, TH - 2 * EDGE + 4
    for i in range(count):
        shifted(comp_ref, top + i, comp3, i)
    groups = [
        ([(comp_ref, top + s + i) for i in range(G1 + 2)], s, s) for s in group_starts(count - 2)
    ]
    first_layer(groups, one_ref, bias_ref, comp3, hid3)
    blocks = [(s, EDGE + s) for s in range(0, TH - 2 * EDGE, 2 * G2)]
    second_layer(blocks, two_ref, bias_ref, hid3, out, out_ref, sems)


def outer_kernel(
    comp_ref, near_ref, far_ref, one_ref, two_ref, bias_ref, inner_ref, out_ref, beside, comp3, hid3, out, sems
):
    del inner_ref
    row_at = lax.axis_index("row")
    odd = row_at % 2
    beside[1 - odd] = near_ref[...]
    beside[odd] = far_ref[...]
    above, below = beside.at[0], beside.at[1]
    upper = [(above, 0), (above, 1)] + [(comp_ref, i) for i in range(EDGE + 2)]
    lower = [(comp_ref, TH - EDGE - 2 + i) for i in range(EDGE + 2)] + [(below, 0), (below, 1)]
    for i, (ref, row) in enumerate(upper + lower):
        shifted(ref, row, comp3, i)
    groups = []
    for part, rows in enumerate((upper, lower)):
        for s in group_starts(EDGE + 2):
            groups.append((rows[s : s + G1 + 2], part * (EDGE + 4) + s, part * (EDGE + 2) + s))
    first_layer(groups, one_ref, bias_ref, comp3, hid3)
    for row, outside in ((0, row_at == 0), (2 * EDGE + 3, row_at == lax.axis_size("row") - 1)):
        x = hid3[row]
        hid3[row] = jnp.where(outside, jnp.zeros_like(x), x)
    second_layer([(0, 0), (EDGE + 2, TH - EDGE)], two_ref, bias_ref, hid3, out, out_ref, sems)


def layer_scratch(rows, parts):
    return [
        pltpu.VMEM((rows + 4 * parts, 3 * FS, TW), BF),
        pltpu.VMEM((rows + 2 * parts, 3 * C, TW), BF),
        pltpu.VMEM((C, rows, TW), BF),
        pltpu.SemaphoreType.DMA((rows // (2 * G2),)),
    ]


def inner(comp, band1, band2, bias):
    rows = TH - 2 * EDGE
    return pl.pallas_call(
        inner_kernel,
        out_specs=pl.BlockSpec(memory_space=pl.ANY),
        out_shape=jax.ShapeDtypeStruct((C, TH, TW), BF),
        scratch_shapes=layer_scratch(rows, 1),
        compiler_params=pltpu.CompilerParams(vmem_limit_bytes=32 << 20),
        cost_estimate=pl.CostEstimate(
            flops=2 * (M1 * K1 + M2 * K2) * TW * 13, bytes_accessed=8_000_000, transcendentals=0
        ),
        name="inner",
    )(comp, band1, band2, bias)


def outer(comp, near, far, band1, band2, bias, inner_rows):
    vmem = pl.BlockSpec(memory_space=pltpu.VMEM)
    return pl.pallas_call(
        outer_kernel,
        in_specs=[vmem] * 6 + [pl.BlockSpec(memory_space=pl.ANY)],
        out_specs=pl.BlockSpec(memory_space=pl.ANY),
        out_shape=jax.ShapeDtypeStruct((C, TH, TW), BF),
        input_output_aliases={6: 0},
        scratch_shapes=[pltpu.VMEM((2, 2, FS, TW + LANES), BF)] + layer_scratch(2 * EDGE, 2),
        compiler_params=pltpu.CompilerParams(vmem_limit_bytes=32 << 20),
        name="outer",
    )(comp, near, far, band1, band2, bias, inner_rows)


def swap(x, axis, first):
    pairs = [(i, i + 1) for i in range(first, lax.axis_size(axis) - 1, 2)]
    return lax.ppermute(x, axis, pairs + [(j, i) for i, j in pairs])


def on_device(
    ray_rows,
    targets,
    cell_block,
    interp_weights,
    first_kernel,
    first_bias,
    second_kernel,
    second_bias,
):
    outgoing, band1, band2, bias = send(
        targets.T,
        cell_block.T,
        ray_rows.transpose(1, 0, 2),
        interp_weights,
        first_kernel.transpose(0, 2, 1),
        second_kernel,
        first_bias.reshape(1, C),
        second_bias.reshape(1, C),
    )
    incoming = lax.all_to_all(outgoing, ("row", "col"), split_axis=0, concat_axis=0, tiled=True)
    comp, near, far = receive(incoming)
    near = swap(near, "row", 0)
    far = swap(far, "row", 1)
    inner_rows = inner(comp, band1, band2, bias)
    return outer(comp, near, far, band1, band2, bias, inner_rows)


def solution(mesh):
    in_specs = (
        P(("row", "col"), None, None),
        P(("row", "col"), None),
        P(("row", "col"), None),
        P(("row", "col"), None, None, None),
        P(),
        P(),
        P(),
        P(),
    )
    out_specs = P(None, "row", "col")
    return jax.shard_map(
        on_device, mesh=mesh, in_specs=in_specs, out_specs=out_specs, check_vma=False
    )
```
